32 devices in a mesh: bx: 4 (over y, core), by: 8 (over z, x).
Axes of the slice: x: 2, y: 2, z: 4, core: 2. Of those that a mesh axis runs over, the one named last changes fastest.
Arguments:
- point_box: int32 [65536, 1], P(('bx', 'by')), may hold values from 0 to 31; in each aligned block of 2048 rows (0 to 2047, 2048 to 4095, ...) at most 128 rows name the same one
- point_offset: int32 [2, 65536], P(None, ('bx', 'by')), may hold values from 0 to 2047
- point_value: float32 [2, 65536], P(None, ('bx', 'by')), may hold values from -0.0625 to 0.0625
- coef: int32 [4], replicated, may hold values from 0 to 31
Outputs:
- weights: float32 [2, 64, 32768], P(None, None, ('bx', 'by'))
The draws below stay inside these ranges and needn't reach their ends.
Inputs may be any that keep to these rules, and one draw needn't show every extreme that they name: `point_box`: the 2048 points of one device name any one box at most 128 times, a bound that some block reaches.
All inputs are finite; a program needn't handle non-finite values.
Results may differ from the reference program's by a relative error of at most 0.0012.
Values sent between devices are 32-bit elements; how exact they have to be, the bound alone decides.
A program may use at most 64 MiB of HBM per device.

```python
import math
import jax
import jax.numpy as jnp
import numpy as np
from jax import lax

N = 16384
ORDER = 8
PTS_DEV = 2048
TGT1 = 32
TGT2 = 32
CAP = 128
POINTS = 65536
N_BX = 4
N_BY = 8
DEVICES = 32


def touch_ends(result, stream_key, smallest, top_value):
    extent = result.shape
    index_at = [jax.random.randint(jax.random.fold_in(stream_key, axis), (), 0, extent[axis]) for axis in range(len(extent))]
    result = result.at[tuple(index_at)].set(smallest)
    longest = extent.index(max(extent))
    index_at[longest] = (index_at[longest] + 1) % extent[longest]
    return result.at[tuple(index_at)].set(top_value)


def level_of(own_key, extent, shards, least, largest):
    loudness, own = 1.0, jax.random.fold_in(own_key, 6)
    for position, shards_of in shards:
        heights = jnp.exp(jax.random.uniform(jax.random.fold_in(own, position), (shards_of,), jnp.float32, least / len(shards), largest / len(shards)))
        loudness = loudness * jnp.repeat(heights, extent[position] // shards_of).reshape([-1 if axis == position else 1 for axis in range(len(extent))])
    return loudness


def deal_out(rng, own, number, rows, number_of, top, bound, skew):
    order = jax.random.permutation(rng, number_of)
    heavy_load, ordinary = load_shares(number_of, rows * top, bound, skew, True), load_shares(number_of, rows * top, bound, skew, False)
    places = jnp.arange(number_of)

    def named(tallies, turn):
        used = int((tallies > 0).sum())
        fixed = max(1, used // 4)
        shifted = fixed + (places - fixed + turn * (used - fixed)) % max(1, number_of - fixed)
        return jnp.zeros((number_of,), jnp.int32).at[order[jnp.where(places < fixed, places, shifted)]].set(jnp.asarray(tallies, jnp.int32))

    tallies = jnp.where(number % 4 == 0, named(heavy_load, number // 4), named(ordinary, number - number // 4 - 1))
    mixed = jax.random.permutation(jax.random.fold_in(own, 3), number_of)
    source_of, sink = mixed[0:number_of // 2 * 2:2], mixed[1:number_of // 2 * 2:2]
    margin = jnp.minimum(tallies[source_of] - 1, bound - tallies[sink]) // 2
    margin = jnp.where((source_of == order[0]) | (sink == order[0]) | (tallies[sink] == 0), 0, jnp.maximum(margin, 0))
    shifted = jax.random.randint(jax.random.fold_in(own, 4), (number_of // 2,), 0, 1 << 20) % (margin + 1)
    tallies = tallies.at[source_of].add(-shifted).at[sink].add(shifted)
    members = jnp.searchsorted(jnp.cumsum(tallies), jnp.arange(rows * top), side="right").astype(jnp.int32)
    listing = members.reshape(top, rows).T
    listing = listing[jax.random.permutation(jax.random.fold_in(own, 1), rows)]
    turn = jax.random.randint(jax.random.fold_in(own, 2), (rows, 1), 0, top)
    return jnp.take_along_axis(listing, (jnp.arange(top)[None, :] + turn) % top, axis=1)


def load_shares(number_of, total, bound, slope, full):
    weights = [(1 << 20) // math.isqrt(rank ** slope) + 1 for rank in range(1, number_of + 1)]
    largest = bound if full else min(bound, max(-(-total // number_of), total * weights[0] // sum(weights)))
    least = 1 if total - largest >= number_of - 1 else 0
    given, spare = [largest] + [least] * (number_of - 1), total - largest - least * (number_of - 1)
    while spare > 0:
        movable = [i for i in range(1, number_of) if given[i] < largest] or [i for i in range(1, number_of) if given[i] < bound]
        whole, left = sum([weights[i] for i in movable]), spare
        for i in movable:
            addition = min(bound - given[i], max(1, left * weights[i] // whole), spare)
            given[i] = given[i] + addition
            spare = spare - addition
    return np.array(given)


def gaussian(rng, extent, scale, limit, pieces=(), held_as=jnp.bfloat16):
    entries = scale * jax.random.normal(rng, extent, jnp.float32)
    if pieces:
        entries = entries * level_of(rng, extent, pieces, -0.22, 0.18)
    return jnp.clip(entries, -limit, limit).astype(held_as)


def setup_inputs(seed: int = 0) -> dict:
    arg_keys = jax.random.split(jax.random.key(seed), 5)
    point_box_keys = jax.random.split(jax.random.fold_in(arg_keys[0], 1), POINTS // PTS_DEV)
    point_box_turns = jax.random.permutation(jax.random.fold_in(arg_keys[0], 3), POINTS // PTS_DEV)
    point_box = jax.vmap(lambda own, number: deal_out(jax.random.fold_in(arg_keys[0], 2), own, number, PTS_DEV, DEVICES, 1, CAP, 2))(point_box_keys, point_box_turns).reshape((POINTS, 1))
    point_offset = touch_ends(jax.random.randint(arg_keys[1], (2, POINTS), 0, N // N_BY), jax.random.fold_in(arg_keys[1], 1), 0, (N // N_BY) - 1).astype(jnp.int32)
    point_value = gaussian(arg_keys[2], (2, POINTS), 0.01, 0.0625, ((1, 32),), jnp.float32)
    coef = touch_ends(jax.random.randint(arg_keys[3], (4,), 0, 32), jax.random.fold_in(arg_keys[3], 1), 0, 31).astype(jnp.int32)
    return {"point_box": point_box, "point_offset": point_offset, "point_value": point_value, "coef": coef}


def node_table():
    counting = np.arange(ORDER) * 1.0
    return 0.5 - 0.5 * np.cos(np.pi * (2.0 * counting + 1.0) / (2.0 * ORDER))

def lagrange(coords):
    nodes = node_table()
    columns = []
    for target in range(ORDER):
        factor = jnp.ones_like(coords)
        for source in range(ORDER):
            if source != target:
                factor = factor * ((coords - float(nodes[source])) * float(1.0 / (nodes[target] - nodes[source])))
        columns.append(factor)
    return jnp.stack(columns, axis=-1)

def child_matrix(side):
    nodes = node_table()
    points = 0.5 * (side + nodes)
    rows_all = []
    for target in range(ORDER):
        factor = np.ones(ORDER)
        for source in range(ORDER):
            if source != target:
                factor = factor * (points - nodes[source]) / (nodes[target] - nodes[source])
        rows_all.append(factor)
    return jnp.asarray(np.stack(rows_all), dtype=jnp.float32)

def phases(tgt_first, tgt_second, freq_first, freq_second, coef):
    scaled = coef.astype(jnp.float32)
    wave = jnp.sin(128.0 * jnp.pi * (tgt_first + tgt_second))
    speed_first = (32.0 + scaled[0] + scaled[1] * wave) / 4096.0
    speed_second = (32.0 + scaled[2] + scaled[3] * wave) / 4096.0
    kfirst = freq_first[:, None]
    ksecond = freq_second[:, None]
    total = tgt_first * kfirst + tgt_second * ksecond + jnp.sqrt(1.0 + (speed_first * kfirst) ** 2 + (speed_second * ksecond) ** 2)
    fraction = total - jnp.floor(total)
    return (jnp.cos(2.0 * jnp.pi * fraction), jnp.sin(2.0 * jnp.pi * fraction))

def grid_nodes(corner_first, width_first, corner_second, width_second):
    nodes = jnp.asarray(node_table(), dtype=jnp.float32)
    along_first = corner_first + width_first * nodes
    along_second = corner_second + width_second * nodes
    return (jnp.broadcast_to(along_first[:, None], (ORDER, ORDER)).reshape(-1), jnp.broadcast_to(along_second[None, :], (ORDER, ORDER)).reshape(-1))

def tgt_axis(index, merged, count, boxes):
    code = jnp.zeros((), jnp.int32)
    for bit in range(merged):
        code = code + (index >> bit & 1) * 2 ** (merged - 1 - bit)
    place = jnp.arange(count, dtype=jnp.int32) * 2 ** merged + code
    return (place.astype(jnp.float32) + 0.5) * (boxes / (N * 2.0 ** merged))

def centers(index_x, index_y, merged_x, merged_y, boxes_x, boxes_y):
    first = tgt_axis(index_x, merged_x, TGT1, boxes_x)
    second = tgt_axis(index_y, merged_y, TGT2, boxes_y)
    return (jnp.broadcast_to(first[:, None], (TGT1, TGT2)).reshape(-1), jnp.broadcast_to(second[None, :], (TGT1, TGT2)).reshape(-1))

def leaf_terms(columns, corner_first, width_first, corner_second, width_second, tgt_first, tgt_second, coef):
    cosine, sine = phases(tgt_first, tgt_second, columns[0], columns[1], coef)
    real_in = columns[2][:, None]
    imag_in = columns[3][:, None]
    real_part = cosine * real_in - sine * imag_in
    imag_part = cosine * imag_in + sine * real_in
    basis_first = lagrange((columns[0] - corner_first) / width_first)
    basis_second = lagrange((columns[1] - corner_second) / width_second)
    basis = (basis_first[:, :, None] * basis_second[:, None, :]).reshape(columns.shape[1], ORDER * ORDER)
    dims = (((0,), (0,)), ((), ()))
    real_sum = lax.dot_general(basis, real_part, dims, precision=lax.Precision.HIGHEST, preferred_element_type=jnp.float32)
    imag_sum = lax.dot_general(basis, imag_part, dims, precision=lax.Precision.HIGHEST, preferred_element_type=jnp.float32)
    return (real_sum, imag_sum)

def shift_back(real_sum, imag_sum, node_first, node_second, tgt_first, tgt_second, coef):
    cosine, sine = phases(tgt_first, tgt_second, node_first, node_second, coef)
    return jnp.stack([cosine * real_sum + sine * imag_sum, cosine * imag_sum - sine * real_sum])

def merge_box(first_w, second_w, tgt_first, tgt_second, along, corner_d, width_d, corner_o, width_o, coef):
    spreads = []
    for side, child in ((0, first_w), (1, second_w)):
        start = corner_d + side * width_d
        if along == 1:
            node_first, node_second = grid_nodes(start, width_d, corner_o, width_o)
        else:
            node_first, node_second = grid_nodes(corner_o, width_o, start, width_d)
        cosine, sine = phases(tgt_first, tgt_second, node_first, node_second, coef)
        lifted = jnp.stack([cosine * child[0] - sine * child[1], cosine * child[1] + sine * child[0]])
        lifted = lifted.reshape(2, ORDER, ORDER, -1)
        table = child_matrix(side)
        if along == 1:
            spreads.append(jnp.einsum('ts,rsuk->rtuk', table, lifted, precision=lax.Precision.HIGHEST))
        else:
            spreads.append(jnp.einsum('us,rtsk->rtuk', table, lifted, precision=lax.Precision.HIGHEST))
    total = (spreads[0] + spreads[1]).reshape(2, ORDER * ORDER, -1)
    if along == 1:
        node_first, node_second = grid_nodes(corner_d, 2.0 * width_d, corner_o, width_o)
    else:
        node_first, node_second = grid_nodes(corner_o, width_o, corner_d, 2.0 * width_d)
    return shift_back(total[0], total[1], node_first, node_second, tgt_first, tgt_second, coef)

def merge_first(holding, partner, index_x, row_y, level, boxes_x, boxes_y, coef):
    width_first = N // boxes_x
    width_second = N // boxes_y
    flag = index_x >> level & 1 == 0
    first_w = jnp.where(flag, holding, partner)
    second_w = jnp.where(flag, partner, holding)
    tgt_first, tgt_second = centers(index_x, row_y, level + 1, level, boxes_x, boxes_y)
    corner_d = ((index_x >> level + 1) * (width_first * 2 ** (level + 1))).astype(jnp.float32)
    corner_o = ((row_y >> level) * (width_second * 2 ** level)).astype(jnp.float32)
    return merge_box(first_w, second_w, tgt_first, tgt_second, 1, corner_d, float(width_first * 2 ** level), corner_o, float(width_second * 2 ** level), coef)

def merge_second(holding, partner, index_x, index_y, level, boxes_x, boxes_y, coef):
    width_first = N // boxes_x
    width_second = N // boxes_y
    flag = index_y >> level & 1 == 0
    first_w = jnp.where(flag, holding, partner)
    second_w = jnp.where(flag, partner, holding)
    tgt_first, tgt_second = centers(index_x, index_y, level + 1, level + 1, boxes_x, boxes_y)
    corner_d = ((index_y >> level + 1) * (width_second * 2 ** (level + 1))).astype(jnp.float32)
    corner_o = ((index_x >> level + 1) * (width_first * 2 ** (level + 1))).astype(jnp.float32)
    return merge_box(first_w, second_w, tgt_first, tgt_second, 2, corner_d, float(width_second * 2 ** level), corner_o, float(width_first * 2 ** (level + 1)), coef)

def pack_slots(box_ids, offsets, values, boxes_y, width_first, width_second, owners, slot_cap):
    ids = box_ids[:, 0]
    onehot = (ids[:, None] == jnp.arange(owners, dtype=jnp.int32)[None, :]).astype(jnp.int32)
    ranks = lax.optimization_barrier(jnp.sum((jnp.cumsum(onehot, axis=0) - 1) * onehot, axis=1))
    freq_first = (ids // boxes_y * width_first + offsets[0]).astype(jnp.float32)
    freq_second = (ids % boxes_y * width_second + offsets[1]).astype(jnp.float32)
    stacked = jnp.stack([freq_first, freq_second, values[0], values[1]], axis=0)
    slot_of = ids * slot_cap + ranks
    blank = jnp.concatenate([jnp.full((2, owners * slot_cap), -1.0, jnp.float32), jnp.zeros((2, owners * slot_cap), jnp.float32)], axis=0)
    filled = blank.at[:, slot_of].set(stacked)
    return filled.reshape(4, owners, slot_cap).transpose(1, 0, 2).reshape(owners, 4 * slot_cap)

def spread_columns(arrived):
    owners = arrived.shape[0]
    return arrived.reshape(owners, 4, -1).transpose(1, 0, 2).reshape(4, -1)

def reference(point_box, point_offset, point_value, coef):
    owners = N_BX * N_BY
    width_first = N // N_BX
    width_second = N // N_BY
    box_rows = point_box.reshape(owners, PTS_DEV, 1)
    offset_rows = point_offset.reshape(2, owners, PTS_DEV).transpose(1, 0, 2)
    value_rows = point_value.reshape(2, owners, PTS_DEV).transpose(1, 0, 2)
    sent = lax.map(lambda group: pack_slots(group[0], group[1], group[2], N_BY, width_first, width_second, owners, CAP), (box_rows, offset_rows, value_rows))
    arrived = sent.transpose(1, 0, 2)

    def leaf_of(group):
        received, owner = group
        index_x = owner // N_BY
        index_y = owner % N_BY
        columns = spread_columns(received)
        corner_first = (index_x * width_first).astype(jnp.float32)
        corner_second = (index_y * width_second).astype(jnp.float32)
        tgt_first, tgt_second = centers(index_x, index_y, 0, 0, N_BX, N_BY)
        real_sum, imag_sum = leaf_terms(columns, corner_first, float(width_first), corner_second, float(width_second), tgt_first, tgt_second, coef)
        node_first, node_second = grid_nodes(corner_first, float(width_first), corner_second, float(width_second))
        return shift_back(real_sum, imag_sum, node_first, node_second, tgt_first, tgt_second, coef)
    weights = lax.map(leaf_of, (arrived, jnp.arange(owners, dtype=jnp.int32)))
    weights = weights.reshape(N_BX, N_BY, 2, ORDER * ORDER, TGT1 * TGT2)
    grid_x = jnp.broadcast_to(jnp.arange(N_BX, dtype=jnp.int32)[:, None], (N_BX, N_BY))
    grid_y = jnp.broadcast_to(jnp.arange(N_BY, dtype=jnp.int32)[None, :], (N_BX, N_BY))
    for level in range(2):
        partner = weights[jnp.arange(N_BX, dtype=jnp.int32) ^ 1 << level]
        step_first = jax.vmap(jax.vmap(lambda hold, other, ix, iy: merge_first(hold, other, ix, iy, level, N_BX, N_BY, coef)))
        weights = step_first(weights, partner, grid_x, grid_y)
        partner = weights[:, jnp.arange(N_BY, dtype=jnp.int32) ^ 1 << level]
        step_second = jax.vmap(jax.vmap(lambda hold, other, ix, iy: merge_second(hold, other, ix, iy, level, N_BX, N_BY, coef)))
        weights = step_second(weights, partner, grid_x, grid_y)
    weights = weights.reshape(owners, 2, ORDER * ORDER, TGT1 * TGT2)
    return weights.transpose(1, 2, 0, 3).reshape(2, ORDER * ORDER, owners * TGT1 * TGT2)
```

```python
import functools

import jax
import jax.numpy as jnp
import numpy as np
from jax import lax
from jax.experimental import pallas as pl
from jax.experimental.pallas import tpu as pltpu
from jax.sharding import PartitionSpec as P

N = 16384
ORDER = 8
NODES = ORDER * ORDER
TGT1 = 32
TGT2 = 32
STEP = 256
UC = 4
CW = UC * TGT2
CHUNKS = TGT1 // UC
HALF = 48
MESH = pl.DeviceIdType.MESH
F32 = jnp.float32
BF16 = jnp.bfloat16
NT = (((1,), (1,)), ((), ()))


def node_table():
    counting = np.arange(ORDER) * 1.0
    return 0.5 - 0.5 * np.cos(np.pi * (2.0 * counting + 1.0) / (2.0 * ORDER))


def child_matrix(side):
    nodes = node_table()
    points = 0.5 * (side + nodes)
    rows_all = []
    for target in range(ORDER):
        factor = np.ones(ORDER)
        for source in range(ORDER):
            if source != target:
                factor = factor * (points - nodes[source]) / (nodes[target] - nodes[source])
        rows_all.append(factor)
    return np.stack(rows_all).astype(np.float32)


def merge_tables():
    eye = np.eye(ORDER, dtype=np.float32)
    first = [np.kron(child_matrix(side), eye) for side in (0, 1)]
    second = [np.kron(eye, child_matrix(side)) for side in (0, 1)]
    return np.stack([np.stack(first), np.stack(second)])


def lagrange_scales():
    nodes = node_table()
    scales = np.ones((ORDER, ORDER))
    for target in range(ORDER):
        for source in range(ORDER):
            if source != target:
                scales[target, source] = 1.0 / (nodes[target] - nodes[source])
    return scales.astype(np.float32)


def sine_coefficients():
    y = 0.25 * np.cos(np.pi * (np.arange(400) + 0.5) / 800)
    target = np.sin(2 * np.pi * y) / y
    fit = np.polynomial.chebyshev.Chebyshev.fit(y * y, target, 5, domain=[0.0, 1.0 / 16.0])
    return [float(c) for c in fit.convert(kind=np.polynomial.Polynomial).coef]


SINE = sine_coefficients()


def quarter_sine(y):
    square = y * y
    value = jnp.full_like(y, SINE[5])
    for c in SINE[4::-1]:
        value = value * square + c
    return value * y


def cos_sin(cycles):
    q = cycles - jnp.round(cycles)
    cosine = quarter_sine(0.25 - jnp.abs(q))
    sine = quarter_sine(jnp.maximum(jnp.minimum(q, 0.5 - q), -0.5 - q))
    return cosine, sine


def split(value):
    high = value.astype(BF16)
    return high, (value - high.astype(F32)).astype(BF16)


def pack_kernel(owners, cap, ids_ref, offset_ref, value_ref, tri_ref, out_ref):
    total = ids_ref.shape[1]
    width = 256
    carry = jnp.zeros((owners, 1), F32)
    packed = jnp.zeros((10 * owners, cap), F32)
    for block in range(total // width):
        lanes = slice(block * width, (block + 1) * width)
        ids = ids_ref[:, lanes]
        hit = ids == lax.broadcasted_iota(jnp.int32, (owners, width), 0)
        onehot = hit.astype(F32)
        before = jnp.dot(onehot.astype(BF16), tri_ref[...], preferred_element_type=F32) + carry
        ranks = jnp.sum(before * onehot, axis=0, keepdims=True)
        carry = carry + jnp.sum(onehot, axis=1, keepdims=True)
        slot = lax.broadcasted_iota(jnp.int32, (cap, width), 0)
        place = (slot == ranks.astype(jnp.int32)).astype(F32).astype(BF16)
        parts = []
        for row in range(2):
            offset = offset_ref[row : row + 1, lanes]
            low = offset & 127
            parts += [(offset - low).astype(F32), low.astype(F32)]
        for row in range(2):
            value = value_ref[row : row + 1, lanes]
            high = value.astype(BF16).astype(F32)
            rest = value - high
            middle = rest.astype(BF16).astype(F32)
            parts += [high, middle, rest - middle]
        lhs = jnp.concatenate([onehot * part for part in parts], axis=0).astype(BF16)
        packed = packed + lax.dot_general(lhs, place, NT, preferred_element_type=F32)
    rows = [packed[i * owners : (i + 1) * owners] for i in range(10)]
    fields = [rows[0] + rows[1], rows[2] + rows[3]]
    fields += [(rows[4] + rows[5]) + rows[6], (rows[7] + rows[8]) + rows[9]]
    for i, field in enumerate(fields):
        out_ref[:, i * cap : (i + 1) * cap] = field


def code_of(index, merged):
    code = index * 0
    for bit in range(merged):
        code = code + (index // 2**bit) % 2 * 2 ** (merged - 1 - bit)
    return code


def flipped(index, level):
    return index + 2**level - 2 * 2**level * ((index // 2**level) % 2)


def main_kernel(
    boxes_x, boxes_y, coef_ref, col_ref, merge_ref, scale_ref, node_ref, out_ref,
    hr_ref, hi_ref, zr_ref, zi_ref, basis_ref, acc_ref, sent_ref, got_ref, send_sem, recv_sem,
):
    ix = lax.axis_index("bx")
    iy = lax.axis_index("by")
    partners = []
    for level in range(2):
        partners.append({"bx": flipped(ix, level), "by": iy})
        partners.append({"bx": ix, "by": flipped(iy, level)})
    barrier = pltpu.get_barrier_semaphore()
    for partner in partners:
        pl.semaphore_signal(barrier, inc=1, device_id=partner, device_id_type=MESH)

    wx = N // boxes_x
    wy = N // boxes_y
    steps = col_ref.shape[0]
    scaled = [coef_ref[i].astype(F32) for i in range(4)]

    def speeds(wave):
        first = (32.0 + scaled[0] + scaled[1] * wave) * (1.0 / 4096.0)
        second = (32.0 + scaled[2] + scaled[3] * wave) * (1.0 / 4096.0)
        return first, second

    row = lax.broadcasted_iota(jnp.int32, (2 * HALF, 1), 0)
    odd = (row >= HALF).astype(jnp.int32)
    m = (2 * (row - HALF * odd) + odd).astype(F32)
    wave = cos_sin(64.0 / N * ((m + 0.5) * boxes_x + 0.5 * boxes_y))[1]
    speed_first, speed_second = speeds(wave)
    sq_first = speed_first * speed_first
    sq_second = speed_second * speed_second
    m_scale = (2.0 * m + 1.0) * (boxes_x / (2.0 * N))
    v_scale = lax.broadcasted_iota(jnp.int32, (TGT2, 1), 0).astype(F32) * (boxes_y / N)
    half_turn = ((ix + iy) % 2).astype(F32) * 0.5
    corner_first = (ix * wx).astype(F32)
    corner_second = (iy * wy).astype(F32)
    node_values = node_table()
    order_row = lax.broadcasted_iota(jnp.int32, (ORDER, 1), 0)

    def lagrange(coords):
        factor = jnp.ones((ORDER, STEP), F32)
        for source in range(ORDER):
            term = (coords - float(node_values[source])) * scale_ref[:, source : source + 1]
            factor = factor * jnp.where(order_row == source, 1.0, term)
        return factor

    def tables(step, carry):
        o1 = col_ref[step, 0:1, :]
        o2 = col_ref[step, 1:2, :]
        re = col_ref[step, 2:3, :]
        im = col_ref[step, 3:4, :]
        k1 = o1 + corner_first
        k2 = o2 + corner_second
        linear = m_scale * o1 + (o2 * (boxes_y / (2.0 * N)) + half_turn)
        root = jnp.sqrt(1.0 + sq_first * (k1 * k1) + sq_second * (k2 * k2))
        cosine, sine = cos_sin((linear - jnp.round(linear)) + root)
        hr_ref[step] = cosine * re - sine * im
        hi_ref[step] = cosine * im + sine * re
        cosine, sine = cos_sin(v_scale * (o2 - o1))
        zr_ref[step] = cosine
        zi_ref[step] = sine
        first = lagrange(o1 * (1.0 / wx))
        second = lagrange(o2 * (1.0 / wy))
        basis = jnp.concatenate([first[t : t + 1] * second for t in range(ORDER)], axis=0)
        high, low = split(basis)
        basis_ref[step] = jnp.concatenate([high, low], axis=0)
        return carry

    lax.fori_loop(0, steps, tables, 0)

    def leaf(chunk):
        def add(step, carry):
            zr = zr_ref[step]
            zi = zi_ref[step]
            reals = []
            imags = []
            for u in range(chunk * UC, (chunk + 1) * UC):
                start = HALF * (u % 2) + u // 2
                hr = hr_ref[step, start : start + TGT2, :]
                hi = hi_ref[step, start : start + TGT2, :]
                reals.append(hr * zr - hi * zi)
                imags.append(hr * zi + hi * zr)
            high, low = split(jnp.concatenate(reals + imags, axis=0))
            basis = basis_ref[step]
            acc_ref[...] += lax.dot_general(
                high, basis, NT, preferred_element_type=F32
            ) + lax.dot_general(low, basis, NT, preferred_element_type=F32)
            return carry

        acc_ref[...] = jnp.zeros_like(acc_ref)
        lax.fori_loop(0, steps, add, 0)
        whole = jnp.transpose(acc_ref[...])
        both = whole[:NODES] + whole[NODES:]
        return both[:, :CW], both[:, CW:]

    lane = lax.broadcasted_iota(jnp.int32, (1, CW), 1)

    def centre(chunk, m1, m2):
        u = (lane // TGT2 + chunk * UC) * 2**m1 + code_of(ix, m1)
        v = lane % TGT2 * 2**m2 + code_of(iy, m2)
        first = (u.astype(F32) + 0.5) * (boxes_x / (N * 2.0**m1))
        second = (v.astype(F32) + 0.5) * (boxes_y / (N * 2.0**m2))
        return first, second

    def roots(place, n1, n2):
        wave = cos_sin(64.0 * (place[0] + place[1]))[1]
        first, second = speeds(wave)
        return jnp.sqrt(1.0 + (first * first) * (n1 * n1) + (second * second) * (n2 * n2))

    def box_nodes(px, py, m1, m2):
        a1 = (px // 2**m1 * (wx * 2**m1)).astype(F32)
        a2 = (py // 2**m2 * (wy * 2**m2)).astype(F32)
        n1 = a1 + float(wx * 2**m1) * node_ref[:, 0:1]
        n2 = a2 + float(wy * 2**m2) * node_ref[:, 1:2]
        return n1, n2

    def merge(chunk, stage, mine, other):
        level, along = stage // 2, stage % 2
        m1, m2 = level + along, level
        new1, new2 = (m1 + 1, m2) if along == 0 else (m1, m2 + 1)
        old_place = centre(chunk, m1, m2)
        new_place = centre(chunk, new1, new2)
        shift1 = (
            (code_of(ix, new1).astype(F32) + 0.5) * (boxes_x / (N * 2.0**new1))
            - (code_of(ix, m1).astype(F32) + 0.5) * (boxes_x / (N * 2.0**m1))
        )
        shift2 = (
            (code_of(iy, new2).astype(F32) + 0.5) * (boxes_y / (N * 2.0**new2))
            - (code_of(iy, m2).astype(F32) + 0.5) * (boxes_y / (N * 2.0**m2))
        )
        px = flipped(ix, level) if along == 0 else ix
        py = flipped(iy, level) if along == 1 else iy
        bit = ((ix if along == 0 else iy) // 2**level) % 2
        lifted = []
        for child, bx, by in ((mine, ix, iy), (other, px, py)):
            n1, n2 = box_nodes(bx, by, m1, m2)
            linear = shift1 * n1 + shift2 * n2
            cycles = (roots(new_place, n1, n2) - roots(old_place, n1, n2)) + linear
            cosine, sine = cos_sin(cycles)
            lifted.append(
                jnp.concatenate(
                    [cosine * child[0] - sine * child[1], cosine * child[1] + sine * child[0]],
                    axis=1,
                )
            )
        low, high = merge_ref[along, 0], merge_ref[along, 1]
        side = bit.astype(F32)
        table_mine = low * (1.0 - side) + high * side
        table_other = low * side + high * (1.0 - side)
        table = jnp.concatenate([table_mine, table_other], axis=1)
        total = jnp.dot(
            table,
            jnp.concatenate(lifted, axis=0),
            precision=lax.Precision.HIGHEST,
            preferred_element_type=F32,
        )
        return total[:, :CW], total[:, CW:]

    def finish(chunk, total):
        place = centre(chunk, 2, 2)
        n1, n2 = box_nodes(ix, iy, 2, 2)
        linear = place[0] * n1 + place[1] * n2
        cosine, sine = cos_sin((linear - jnp.round(linear)) + roots(place, n1, n2))
        lanes = slice(chunk * CW, (chunk + 1) * CW)
        out_ref[0, :, lanes] = cosine * total[0] + sine * total[1]
        out_ref[1, :, lanes] = cosine * total[1] - sine * total[0]

    def exchange(stage, chunk):
        return pltpu.make_async_remote_copy(
            src_ref=sent_ref.at[stage, chunk],
            dst_ref=got_ref.at[stage, chunk],
            send_sem=send_sem.at[stage, chunk],
            recv_sem=recv_sem.at[stage, chunk],
            device_id=partners[stage],
            device_id_type=MESH,
        )

    def send(stage, chunk, value):
        sent_ref[stage, chunk, 0] = value[0]
        sent_ref[stage, chunk, 1] = value[1]
        exchange(stage, chunk).start()

    greeted = False
    for slot in range(CHUNKS + 4):
        if slot < CHUNKS:
            value = leaf(slot)
            if not greeted:
                pl.semaphore_wait(barrier, 4)
                greeted = True
            send(0, slot, value)
        for stage in range(3, -1, -1):
            chunk = slot - 1 - stage
            if 0 <= chunk < CHUNKS:
                exchange(stage, chunk).wait()
                value = merge(chunk, stage, sent_ref.at[stage, chunk], got_ref.at[stage, chunk])
                if stage < 3:
                    send(stage + 1, chunk, value)
                else:
                    finish(chunk, value)


def on_device(point_box, point_offset, point_value, coef):
    boxes_x = lax.axis_size("bx")
    boxes_y = lax.axis_size("by")
    assert boxes_y == 2 * boxes_x
    owners = boxes_x * boxes_y
    held = point_box.shape[0]
    cap = 2 * held // owners
    vmem = pl.BlockSpec(memory_space=pltpu.VMEM)
    tri = jnp.asarray(np.triu(np.ones((256, 256), np.float32), 1), BF16)
    sent = pl.pallas_call(
        functools.partial(pack_kernel, owners, cap),
        out_shape=jax.ShapeDtypeStruct((owners, 4 * cap), F32),
        in_specs=[vmem] * 4,
        out_specs=vmem,
        compiler_params=pltpu.CompilerParams(vmem_limit_bytes=16 << 20),
        name="pack",
    )(point_box.reshape(1, held), point_offset, point_value, tri)
    arrived = lax.all_to_all(sent, ("bx", "by"), split_axis=0, concat_axis=0, tiled=True)
    slots = owners * cap
    steps = slots // STEP
    columns = arrived.reshape(owners, 4, cap).transpose(1, 0, 2).reshape(4, steps, STEP)
    columns = columns.transpose(1, 0, 2)
    nodes = node_table().astype(np.float32)
    node_pairs = np.stack([np.repeat(nodes, ORDER), np.tile(nodes, ORDER)], axis=1)
    return pl.pallas_call(
        functools.partial(main_kernel, boxes_x, boxes_y),
        out_shape=jax.ShapeDtypeStruct((2, NODES, TGT1 * TGT2), F32),
        in_specs=[pl.BlockSpec(memory_space=pltpu.SMEM)] + [vmem] * 4,
        out_specs=vmem,
        scratch_shapes=[
            pltpu.VMEM((steps, 2 * HALF, STEP), F32),
            pltpu.VMEM((steps, 2 * HALF, STEP), F32),
            pltpu.VMEM((steps, TGT2, STEP), F32),
            pltpu.VMEM((steps, TGT2, STEP), F32),
            pltpu.VMEM((steps, 2 * NODES, STEP), BF16),
            pltpu.VMEM((2 * CW, 2 * NODES), F32),
            pltpu.VMEM((4, CHUNKS, 2, NODES, CW), F32),
            pltpu.VMEM((4, CHUNKS, 2, NODES, CW), F32),
            pltpu.SemaphoreType.DMA((4, CHUNKS)),
            pltpu.SemaphoreType.DMA((4, CHUNKS)),
        ],
        compiler_params=pltpu.CompilerParams(
            collective_id=0, has_side_effects=True, vmem_limit_bytes=40 << 20
        ),
        name="butterfly",
    )(coef, columns, jnp.asarray(merge_tables()), jnp.asarray(lagrange_scales()), jnp.asarray(node_pairs))


def solution(mesh):
    in_specs = (P(("bx", "by"), None), P(None, ("bx", "by")), P(None, ("bx", "by")), P())
    out_specs = P(None, None, ("bx", "by"))
    return jax.shard_map(
        on_device, mesh=mesh, in_specs=in_specs, out_specs=out_specs, check_vma=False
    )
```

```python
import functools

import jax
import jax.numpy as jnp
import numpy as np
from jax import lax
from jax.experimental import pallas as pl
from jax.experimental.pallas import tpu as pltpu
from jax.sharding import PartitionSpec as P

N = 16384
ORDER = 8
NODES = ORDER * ORDER
TGT1 = 32
TGT2 = 32
STEP = 256
UC = 4
CW = UC * TGT2
CHUNKS = TGT1 // UC
GROUP = 2
GU = GROUP * UC
GW = GROUP * CW
UNROLL = 2
HALF = 48
MESH = pl.DeviceIdType.MESH
F32 = jnp.float32
BF16 = jnp.bfloat16
NT = (((1,), (1,)), ((), ()))


def node_table():
    counting = np.arange(ORDER) * 1.0
    return 0.5 - 0.5 * np.cos(np.pi * (2.0 * counting + 1.0) / (2.0 * ORDER))


def child_matrix(side):
    nodes = node_table()
    points = 0.5 * (side + nodes)
    rows_all = []
    for target in range(ORDER):
        factor = np.ones(ORDER)
        for source in range(ORDER):
            if source != target:
                factor = factor * (points - nodes[source]) / (nodes[target] - nodes[source])
        rows_all.append(factor)
    return np.stack(rows_all).astype(np.float32)


def merge_tables():
    eye = np.eye(ORDER, dtype=np.float32)
    first = [np.kron(child_matrix(side), eye) for side in (0, 1)]
    second = [np.kron(eye, child_matrix(side)) for side in (0, 1)]
    return np.stack([np.stack(first), np.stack(second)])


def lagrange_scales():
    nodes = node_table()
    scales = np.ones((ORDER, ORDER))
    for target in range(ORDER):
        for source in range(ORDER):
            if source != target:
                scales[target, source] = 1.0 / (nodes[target] - nodes[source])
    return scales.astype(np.float32)


def sine_coefficients():
    y = 0.25 * np.cos(np.pi * (np.arange(400) + 0.5) / 800)
    target = np.sin(2 * np.pi * y) / y
    fit = np.polynomial.chebyshev.Chebyshev.fit(y * y, target, 5, domain=[0.0, 1.0 / 16.0])
    return [float(c) for c in fit.convert(kind=np.polynomial.Polynomial).coef]


SINE = sine_coefficients()


def quarter_sine(y):
    square = y * y
    value = jnp.full_like(y, SINE[5])
    for c in SINE[4::-1]:
        value = value * square + c
    return value * y


def cos_sin(cycles):
    q = cycles - jnp.round(cycles)
    cosine = quarter_sine(0.25 - jnp.abs(q))
    sine = quarter_sine(jnp.maximum(jnp.minimum(q, 0.5 - q), -0.5 - q))
    return cosine, sine


def split(value):
    high = value.astype(BF16)
    return high, (value - high.astype(F32)).astype(BF16)


def pack_kernel(
    boxes_y, owners, cap, ids_ref, offset_ref, value_ref, tri_ref, out_ref,
    sent_ref, got_ref, send_sem, recv_sem,
):
    me = lax.axis_index("bx") * boxes_y + lax.axis_index("by")
    barrier = pltpu.get_barrier_semaphore()

    def place_of(distance):
        target = (me + distance) % owners
        return target, {"bx": target // boxes_y, "by": target % boxes_y}

    def greet(distance, carry):
        where = place_of(distance)[1]
        pl.semaphore_signal(barrier, inc=1, device_id=where, device_id_type=MESH)
        return carry

    lax.fori_loop(1, owners, greet, 0)
    total = ids_ref.shape[1]
    width = 256
    carry = jnp.zeros((owners, 1), F32)
    packed = jnp.zeros((10 * owners, cap), F32)
    for block in range(total // width):
        lanes = slice(block * width, (block + 1) * width)
        ids = ids_ref[:, lanes]
        hit = ids == lax.broadcasted_iota(jnp.int32, (owners, width), 0)
        onehot = hit.astype(F32)
        before = jnp.dot(onehot.astype(BF16), tri_ref[...], preferred_element_type=F32) + carry
        ranks = jnp.sum(before * onehot, axis=0, keepdims=True)
        carry = carry + jnp.sum(onehot, axis=1, keepdims=True)
        slot = lax.broadcasted_iota(jnp.int32, (cap, width), 0)
        place = (slot == ranks.astype(jnp.int32)).astype(F32).astype(BF16)
        parts = []
        for row in range(2):
            offset = offset_ref[row : row + 1, lanes]
            low = offset & 127
            parts += [(offset - low).astype(F32), low.astype(F32)]
        for row in range(2):
            value = value_ref[row : row + 1, lanes]
            high = value.astype(BF16).astype(F32)
            rest = value - high
            middle = rest.astype(BF16).astype(F32)
            parts += [high, middle, rest - middle]
        lhs = jnp.concatenate([onehot * part for part in parts], axis=0).astype(BF16)
        packed = packed + lax.dot_general(lhs, place, NT, preferred_element_type=F32)
    rows = [packed[i * owners : (i + 1) * owners] for i in range(10)]
    fields = [rows[0] + rows[1], rows[2] + rows[3]]
    fields += [(rows[4] + rows[5]) + rows[6], (rows[7] + rows[8]) + rows[9]]
    joined = jnp.concatenate(fields, axis=1)
    for i in range(4 * cap // 128):
        sent_ref[:, i, :] = joined[:, i * 128 : (i + 1) * 128]

    def copy(distance):
        target, where = place_of(distance)
        return pltpu.make_async_remote_copy(
            src_ref=sent_ref.at[target],
            dst_ref=got_ref.at[me],
            send_sem=send_sem.at[distance],
            recv_sem=recv_sem.at[distance],
            device_id=where,
            device_id_type=MESH,
        )

    def begin(distance, carry):
        copy(distance).start()
        return carry

    def end(distance, carry):
        copy(distance).wait()
        return carry

    pl.semaphore_wait(barrier, owners - 1)
    lax.fori_loop(1, owners, begin, 0)
    got_ref[me] = sent_ref[me]
    lax.fori_loop(1, owners, end, 0)
    out_ref[...] = got_ref[...]


def code_of(index, merged):
    code = index * 0
    for bit in range(merged):
        code = code + (index // 2**bit) % 2 * 2 ** (merged - 1 - bit)
    return code


def flipped(index, level):
    return index + 2**level - 2 * 2**level * ((index // 2**level) % 2)


def main_kernel(
    boxes_x, boxes_y, coef_ref, col_ref, merge_ref, scale_ref, node_ref, out_ref,
    hr_ref, hi_ref, zr_ref, zi_ref, basis_ref, acc_ref, sent_ref, got_ref, send_sem, recv_sem,
):
    ix = lax.axis_index("bx")
    iy = lax.axis_index("by")
    partners = []
    for level in range(2):
        partners.append({"bx": flipped(ix, level), "by": iy})
        partners.append({"bx": ix, "by": flipped(iy, level)})
    barrier = pltpu.get_barrier_semaphore()
    for partner in partners:
        pl.semaphore_signal(barrier, inc=1, device_id=partner, device_id_type=MESH)

    wx = N // boxes_x
    wy = N // boxes_y
    steps = col_ref.shape[0]
    scaled = [coef_ref[i].astype(F32) for i in range(4)]

    def speeds(wave):
        first = (32.0 + scaled[0] + scaled[1] * wave) * (1.0 / 4096.0)
        second = (32.0 + scaled[2] + scaled[3] * wave) * (1.0 / 4096.0)
        return first, second

    row = lax.broadcasted_iota(jnp.int32, (2 * HALF, 1), 0)
    odd = (row >= HALF).astype(jnp.int32)
    m = (2 * (row - HALF * odd) + odd).astype(F32)
    wave = cos_sin(64.0 / N * ((m + 0.5) * boxes_x + 0.5 * boxes_y))[1]
    speed_first, speed_second = speeds(wave)
    sq_first = speed_first * speed_first
    sq_second = speed_second * speed_second
    m_scale = (2.0 * m + 1.0) * (boxes_x / (2.0 * N))
    v_scale = lax.broadcasted_iota(jnp.int32, (TGT2, 1), 0).astype(F32) * (boxes_y / N)
    half_turn = ((ix + iy) % 2).astype(F32) * 0.5
    corner_first = (ix * wx).astype(F32)
    corner_second = (iy * wy).astype(F32)
    node_values = node_table()
    order_row = lax.broadcasted_iota(jnp.int32, (ORDER, 1), 0)

    def lagrange(coords):
        factor = jnp.ones((ORDER, STEP), F32)
        for source in range(ORDER):
            term = (coords - float(node_values[source])) * scale_ref[:, source : source + 1]
            factor = factor * jnp.where(order_row == source, 1.0, term)
        return factor

    def tables(step, carry):
        o1 = col_ref[step, 0:1, :]
        o2 = col_ref[step, 1:2, :]
        re = col_ref[step, 2:3, :]
        im = col_ref[step, 3:4, :]
        k1 = o1 + corner_first
        k2 = o2 + corner_second
        linear = m_scale * o1 + (o2 * (boxes_y / (2.0 * N)) + half_turn)
        root = jnp.sqrt(1.0 + sq_first * (k1 * k1) + sq_second * (k2 * k2))
        cosine, sine = cos_sin((linear - jnp.round(linear)) + root)
        hr_ref[step] = cosine * re - sine * im
        hi_ref[step] = cosine * im + sine * re
        cosine, sine = cos_sin(v_scale * (o2 - o1))
        zr_ref[step] = cosine
        zi_ref[step] = sine
        first = lagrange(o1 * (1.0 / wx))
        second = lagrange(o2 * (1.0 / wy))
        basis = jnp.concatenate([first[t : t + 1] * second for t in range(ORDER)], axis=0)
        high, low = split(basis)
        both = jnp.concatenate([high.astype(F32), low.astype(F32)], axis=0)
        basis_ref[step] = jnp.transpose(both).astype(BF16)
        return carry

    lax.fori_loop(0, steps, tables, 0)

    def leaf(group):
        def add(block, carry):
            part = jnp.zeros((2 * GW, 2 * NODES), F32)
            for inner in range(UNROLL):
                step = block * UNROLL + inner
                zr = zr_ref[step]
                zi = zi_ref[step]
                reals = []
                imags = []
                for u in range(group * GU, (group + 1) * GU):
                    start = HALF * (u % 2) + u // 2
                    hr = hr_ref[step, start : start + TGT2, :]
                    hi = hi_ref[step, start : start + TGT2, :]
                    reals.append(hr * zr - hi * zi)
                    imags.append(hr * zi + hi * zr)
                high, low = split(jnp.concatenate(reals + imags, axis=0))
                basis = basis_ref[step]
                part = part + jnp.dot(high, basis, preferred_element_type=F32)
                part = part + jnp.dot(low, basis, preferred_element_type=F32)
            acc_ref[...] += part
            return carry

        acc_ref[...] = jnp.zeros_like(acc_ref)
        lax.fori_loop(0, steps // UNROLL, add, 0)
        whole = jnp.transpose(acc_ref[...])
        both = whole[:NODES] + whole[NODES:]
        return [
            (both[:, i * CW : (i + 1) * CW], both[:, GW + i * CW : GW + (i + 1) * CW])
            for i in range(GROUP)
        ]

    lane = lax.broadcasted_iota(jnp.int32, (1, CW), 1)

    def centre(chunk, m1, m2):
        u = (lane // TGT2 + chunk * UC) * 2**m1 + code_of(ix, m1)
        v = lane % TGT2 * 2**m2 + code_of(iy, m2)
        first = (u.astype(F32) + 0.5) * (boxes_x / (N * 2.0**m1))
        second = (v.astype(F32) + 0.5) * (boxes_y / (N * 2.0**m2))
        return first, second

    def roots(place, n1, n2):
        wave = cos_sin(64.0 * (place[0] + place[1]))[1]
        first, second = speeds(wave)
        return jnp.sqrt(1.0 + (first * first) * (n1 * n1) + (second * second) * (n2 * n2))

    def box_nodes(px, py, m1, m2):
        a1 = (px // 2**m1 * (wx * 2**m1)).astype(F32)
        a2 = (py // 2**m2 * (wy * 2**m2)).astype(F32)
        n1 = a1 + float(wx * 2**m1) * node_ref[:, 0:1]
        n2 = a2 + float(wy * 2**m2) * node_ref[:, 1:2]
        return n1, n2

    def merge(chunk, stage, mine, other):
        level, along = stage // 2, stage % 2
        m1, m2 = level + along, level
        new1, new2 = (m1 + 1, m2) if along == 0 else (m1, m2 + 1)
        old_place = centre(chunk, m1, m2)
        new_place = centre(chunk, new1, new2)
        shift1 = (
            (code_of(ix, new1).astype(F32) + 0.5) * (boxes_x / (N * 2.0**new1))
            - (code_of(ix, m1).astype(F32) + 0.5) * (boxes_x / (N * 2.0**m1))
        )
        shift2 = (
            (code_of(iy, new2).astype(F32) + 0.5) * (boxes_y / (N * 2.0**new2))
            - (code_of(iy, m2).astype(F32) + 0.5) * (boxes_y / (N * 2.0**m2))
        )
        px = flipped(ix, level) if along == 0 else ix
        py = flipped(iy, level) if along == 1 else iy
        bit = ((ix if along == 0 else iy) // 2**level) % 2
        lifted = []
        for child, bx, by in ((mine, ix, iy), (other, px, py)):
            n1, n2 = box_nodes(bx, by, m1, m2)
            linear = shift1 * n1 + shift2 * n2
            cycles = (roots(new_place, n1, n2) - roots(old_place, n1, n2)) + linear
            cosine, sine = cos_sin(cycles)
            lifted.append(
                jnp.concatenate(
                    [cosine * child[0] - sine * child[1], cosine * child[1] + sine * child[0]],
                    axis=1,
                )
            )
        low, high = merge_ref[along, 0], merge_ref[along, 1]
        side = bit.astype(F32)
        table_mine = low * (1.0 - side) + high * side
        table_other = low * side + high * (1.0 - side)
        table = jnp.concatenate([table_mine, table_other], axis=1)
        table_high, table_low = split(table)
        high, low = split(jnp.concatenate(lifted, axis=0))
        total = jnp.dot(table_high, high, preferred_element_type=F32)
        total = total + jnp.dot(table_low, high, preferred_element_type=F32)
        total = total + jnp.dot(table_high, low, preferred_element_type=F32)
        return total[:, :CW], total[:, CW:]

    def finish(chunk, total):
        place = centre(chunk, 2, 2)
        n1, n2 = box_nodes(ix, iy, 2, 2)
        linear = place[0] * n1 + place[1] * n2
        cosine, sine = cos_sin((linear - jnp.round(linear)) + roots(place, n1, n2))
        lanes = slice(chunk * CW, (chunk + 1) * CW)
        out_ref[0, :, lanes] = cosine * total[0] + sine * total[1]
        out_ref[1, :, lanes] = cosine * total[1] - sine * total[0]

    def exchange(stage, chunk):
        return pltpu.make_async_remote_copy(
            src_ref=sent_ref.at[stage, chunk],
            dst_ref=got_ref.at[stage, chunk],
            send_sem=send_sem.at[stage, chunk],
            recv_sem=recv_sem.at[stage, chunk],
            device_id=partners[stage],
            device_id_type=MESH,
        )

    def send(stage, chunk, value):
        sent_ref[stage, chunk, 0] = value[0]
        sent_ref[stage, chunk, 1] = value[1]
        exchange(stage, chunk).start()

    greeted = False
    groups = CHUNKS // GROUP
    for slot in range(groups + 4):
        if slot < groups:
            values = leaf(slot)
            if not greeted:
                pl.semaphore_wait(barrier, 4)
                greeted = True
            for i in range(GROUP):
                send(0, slot * GROUP + i, values[i])
        for stage in range(3, -1, -1):
            group = slot - 1 - stage
            if 0 <= group < groups:
                for chunk in range(group * GROUP, (group + 1) * GROUP):
                    exchange(stage, chunk).wait()
                    value = merge(chunk, stage, sent_ref.at[stage, chunk], got_ref.at[stage, chunk])
                    if stage < 3:
                        send(stage + 1, chunk, value)
                    else:
                        finish(chunk, value)


def on_device(point_box, point_offset, point_value, coef):
    boxes_x = lax.axis_size("bx")
    boxes_y = lax.axis_size("by")
    assert boxes_y == 2 * boxes_x
    owners = boxes_x * boxes_y
    held = point_box.shape[0]
    cap = 2 * held // owners
    vmem = pl.BlockSpec(memory_space=pltpu.VMEM)
    tri = jnp.asarray(np.triu(np.ones((256, 256), np.float32), 1), BF16)
    block = (owners, 4 * cap // 128, 128)
    arrived = pl.pallas_call(
        functools.partial(pack_kernel, boxes_y, owners, cap),
        out_shape=jax.ShapeDtypeStruct(block, F32),
        in_specs=[vmem] * 4,
        out_specs=vmem,
        scratch_shapes=[
            pltpu.VMEM(block, F32),
            pltpu.VMEM(block, F32),
            pltpu.SemaphoreType.DMA((owners,)),
            pltpu.SemaphoreType.DMA((owners,)),
        ],
        compiler_params=pltpu.CompilerParams(
            collective_id=1, has_side_effects=True, vmem_limit_bytes=16 << 20
        ),
        name="pack",
    )(point_box.reshape(1, held), point_offset, point_value, tri)
    slots = owners * cap
    steps = slots // STEP
    columns = arrived.reshape(owners, 4, cap).transpose(1, 0, 2).reshape(4, steps, STEP)
    columns = columns.transpose(1, 0, 2)
    nodes = node_table().astype(np.float32)
    node_pairs = np.stack([np.repeat(nodes, ORDER), np.tile(nodes, ORDER)], axis=1)
    return pl.pallas_call(
        functools.partial(main_kernel, boxes_x, boxes_y),
        out_shape=jax.ShapeDtypeStruct((2, NODES, TGT1 * TGT2), F32),
        in_specs=[pl.BlockSpec(memory_space=pltpu.SMEM)] + [vmem] * 4,
        out_specs=vmem,
        scratch_shapes=[
            pltpu.VMEM((steps, 2 * HALF, STEP), F32),
            pltpu.VMEM((steps, 2 * HALF, STEP), F32),
            pltpu.VMEM((steps, TGT2, STEP), F32),
            pltpu.VMEM((steps, TGT2, STEP), F32),
            pltpu.VMEM((steps, STEP, 2 * NODES), BF16),
            pltpu.VMEM((2 * GW, 2 * NODES), F32),
            pltpu.VMEM((4, CHUNKS, 2, NODES, CW), F32),
            pltpu.VMEM((4, CHUNKS, 2, NODES, CW), F32),
            pltpu.SemaphoreType.DMA((4, CHUNKS)),
            pltpu.SemaphoreType.DMA((4, CHUNKS)),
        ],
        compiler_params=pltpu.CompilerParams(
            collective_id=0, has_side_effects=True, vmem_limit_bytes=40 << 20
        ),
        name="butterfly",
    )(coef, columns, jnp.asarray(merge_tables()), jnp.asarray(lagrange_scales()), jnp.asarray(node_pairs))


def solution(mesh):
    in_specs = (P(("bx", "by"), None), P(None, ("bx", "by")), P(None, ("bx", "by")), P())
    out_specs = P(None, None, ("bx", "by"))
    return jax.shard_map(
        on_device, mesh=mesh, in_specs=in_specs, out_specs=out_specs, check_vma=False
    )
```

```python
import functools

import jax
import jax.numpy as jnp
import numpy as np
from jax import lax
from jax.experimental import pallas as pl
from jax.experimental.pallas import tpu as pltpu
from jax.sharding import PartitionSpec as P

N = 16384
ORDER = 8
NODES = ORDER * ORDER
TGT1 = 32
TGT2 = 32
STEP = 256
UC = 4
CW = UC * TGT2
CHUNKS = TGT1 // UC
GROUP = 2
GROUPS = CHUNKS // GROUP
WRAP = 24
UNROLL = 2
HALF = 48
MESH = pl.DeviceIdType.MESH
F32 = jnp.float32
BF16 = jnp.bfloat16
NT = (((1,), (1,)), ((), ()))


def node_table():
    counting = np.arange(ORDER) * 1.0
    return 0.5 - 0.5 * np.cos(np.pi * (2.0 * counting + 1.0) / (2.0 * ORDER))


def child_matrix(side):
    nodes = node_table()
    points = 0.5 * (side + nodes)
    rows_all = []
    for target in range(ORDER):
        factor = np.ones(ORDER)
        for source in range(ORDER):
            if source != target:
                factor = factor * (points - nodes[source]) / (nodes[target] - nodes[source])
        rows_all.append(factor)
    return np.stack(rows_all).astype(np.float32)


def merge_tables():
    eye = np.eye(ORDER, dtype=np.float32)
    first = [np.kron(child_matrix(side), eye) for side in (0, 1)]
    second = [np.kron(eye, child_matrix(side)) for side in (0, 1)]
    return np.stack([np.stack(first), np.stack(second)])


def lagrange_scales():
    nodes = node_table()
    scales = np.ones((ORDER, ORDER))
    for target in range(ORDER):
        for source in range(ORDER):
            if source != target:
                scales[target, source] = 1.0 / (nodes[target] - nodes[source])
    return scales.astype(np.float32)


def sine_coefficients():
    y = 0.25 * np.cos(np.pi * (np.arange(400) + 0.5) / 800)
    target = np.sin(2 * np.pi * y) / y
    fit = np.polynomial.chebyshev.Chebyshev.fit(y * y, target, 5, domain=[0.0, 1.0 / 16.0])
    return [float(c) for c in fit.convert(kind=np.polynomial.Polynomial).coef]


SINE = sine_coefficients()


def quarter_sine(y):
    square = y * y
    value = jnp.full_like(y, SINE[5])
    for c in SINE[4::-1]:
        value = value * square + c
    return value * y


def cos_sin(cycles):
    q = cycles - jnp.round(cycles)
    cosine = quarter_sine(0.25 - jnp.abs(q))
    sine = quarter_sine(jnp.maximum(jnp.minimum(q, 0.5 - q), -0.5 - q))
    return cosine, sine


def split(value):
    high = value.astype(BF16)
    return high, (value - high.astype(F32)).astype(BF16)


def pack_kernel(
    boxes_y, owners, cap, ids_hbm, offset_hbm, value_hbm, out_ref,
    ids_ref, offset_ref, value_ref, sent_ref, got_ref, load_sem, send_sem, recv_sem,
):
    me = lax.axis_index("bx") * boxes_y + lax.axis_index("by")
    barrier = pltpu.get_barrier_semaphore()
    loads = [
        pltpu.make_async_copy(ids_hbm, ids_ref, load_sem.at[0]),
        pltpu.make_async_copy(offset_hbm, offset_ref, load_sem.at[1]),
        pltpu.make_async_copy(value_hbm, value_ref, load_sem.at[2]),
    ]
    for load in loads:
        load.start()

    def place_of(distance):
        target = (me + distance) % owners
        return target, {"bx": target // boxes_y, "by": target % boxes_y}

    def greet(distance, carry):
        where = place_of(distance)[1]
        pl.semaphore_signal(barrier, inc=1, device_id=where, device_id_type=MESH)
        return carry

    lax.fori_loop(1, owners, greet, 0)
    total = ids_ref.shape[1]
    width = 256
    earlier = lax.broadcasted_iota(jnp.int32, (width, width), 0)
    later = lax.broadcasted_iota(jnp.int32, (width, width), 1)
    tri = (earlier < later).astype(F32).astype(BF16)
    carry = jnp.zeros((owners, 1), F32)
    for load in loads:
        load.wait()
    packed = jnp.zeros((10 * owners, cap), F32)
    for block in range(total // width):
        lanes = slice(block * width, (block + 1) * width)
        ids = ids_ref[:, lanes]
        hit = ids == lax.broadcasted_iota(jnp.int32, (owners, width), 0)
        onehot = hit.astype(F32)
        before = jnp.dot(onehot.astype(BF16), tri, preferred_element_type=F32) + carry
        ranks = jnp.sum(before * onehot, axis=0, keepdims=True)
        carry = carry + jnp.sum(onehot, axis=1, keepdims=True)
        slot = lax.broadcasted_iota(jnp.int32, (cap, width), 0)
        place = (slot == ranks.astype(jnp.int32)).astype(F32).astype(BF16)
        parts = []
        for row in range(2):
            offset = offset_ref[row : row + 1, lanes]
            low = offset & 127
            parts += [(offset - low).astype(F32), low.astype(F32)]
        for row in range(2):
            value = value_ref[row : row + 1, lanes]
            high = value.astype(BF16).astype(F32)
            rest = value - high
            middle = rest.astype(BF16).astype(F32)
            parts += [high, middle, rest - middle]
        lhs = jnp.concatenate([onehot * part for part in parts], axis=0).astype(BF16)
        packed = packed + lax.dot_general(lhs, place, NT, preferred_element_type=F32)
    rows = [packed[i * owners : (i + 1) * owners] for i in range(10)]
    fields = [rows[0] + rows[1], rows[2] + rows[3]]
    fields += [(rows[4] + rows[5]) + rows[6], (rows[7] + rows[8]) + rows[9]]
    joined = jnp.concatenate(fields, axis=1)
    for i in range(4 * cap // 128):
        sent_ref[:, i, :] = joined[:, i * 128 : (i + 1) * 128]

    def copy(distance):
        target, where = place_of(distance)
        return pltpu.make_async_remote_copy(
            src_ref=sent_ref.at[target],
            dst_ref=got_ref.at[me],
            send_sem=send_sem.at[distance],
            recv_sem=recv_sem.at[distance],
            device_id=where,
            device_id_type=MESH,
        )

    def begin(distance, carry):
        copy(distance).start()
        return carry

    def end(distance, carry):
        copy(distance).wait()
        return carry

    pl.semaphore_wait(barrier, owners - 1)
    lax.fori_loop(1, owners, begin, 0)
    got_ref[me] = sent_ref[me]
    lax.fori_loop(1, owners, end, 0)
    out_ref[...] = got_ref[...]


def code_of(index, merged):
    code = index * 0
    for bit in range(merged):
        code = code + (index // 2**bit) % 2 * 2 ** (merged - 1 - bit)
    return code


def flipped(index, level):
    return index + 2**level - 2 * 2**level * ((index // 2**level) % 2)


def main_kernel(
    boxes_x, boxes_y, coef_ref, col_ref, merge_ref, out_ref,
    hr_ref, hi_ref, zr_ref, zi_ref, basis_ref, acc_ref, sent_ref, got_ref, send_sem, recv_sem,
):
    ix = lax.axis_index("bx")
    iy = lax.axis_index("by")
    partners = []
    for level in range(2):
        partners.append({"bx": flipped(ix, level), "by": iy})
        partners.append({"bx": ix, "by": flipped(iy, level)})
    barrier = pltpu.get_barrier_semaphore()
    for partner in partners:
        pl.semaphore_signal(barrier, inc=1, device_id=partner, device_id_type=MESH)

    wx = N // boxes_x
    wy = N // boxes_y
    steps = col_ref.shape[0]
    scaled = [coef_ref[i].astype(F32) for i in range(4)]

    def speeds(wave):
        first = (32.0 + scaled[0] + scaled[1] * wave) * (1.0 / 4096.0)
        second = (32.0 + scaled[2] + scaled[3] * wave) * (1.0 / 4096.0)
        return first, second

    row = lax.broadcasted_iota(jnp.int32, (2 * HALF, 1), 0)
    odd = (row >= HALF).astype(jnp.int32)
    m = (2 * (row - HALF * odd) + odd).astype(F32)
    wave = cos_sin(64.0 / N * ((m + 0.5) * boxes_x + 0.5 * boxes_y))[1]
    speed_first, speed_second = speeds(wave)
    sq_first = speed_first * speed_first
    sq_second = speed_second * speed_second
    m_scale = (2.0 * m + 1.0) * (boxes_x / (2.0 * N))
    v_row = lax.broadcasted_iota(jnp.int32, (TGT2, 1), 0)
    unit = boxes_y / N
    v_first = (v_row + 4).astype(F32) * unit
    v_second = jnp.where(v_row < WRAP, v_row + 4, v_row - 12).astype(F32) * unit
    half_turn = ((ix + iy) % 2).astype(F32) * 0.5
    corner_first = (ix * wx).astype(F32)
    corner_second = (iy * wy).astype(F32)
    node_values = node_table()
    order_row = lax.broadcasted_iota(jnp.int32, (ORDER, 1), 0)

    scales = lagrange_scales()

    def column(values):
        chosen = jnp.full((ORDER, 1), float(values[0]), F32)
        for i in range(1, ORDER):
            chosen = jnp.where(order_row == i, float(values[i]), chosen)
        return chosen

    scale_columns = [column(scales[:, source]) for source in range(ORDER)]
    tile_nodes = column(node_values)
    second_nodes = jnp.concatenate([tile_nodes] * ORDER, axis=0)
    first_nodes = jnp.concatenate(
        [jnp.full((ORDER, 1), float(node_values[t]), F32) for t in range(ORDER)], axis=0
    )

    def lagrange(coords):
        factor = jnp.ones((ORDER, STEP), F32)
        for source in range(ORDER):
            term = (coords - float(node_values[source])) * scale_columns[source]
            factor = factor * jnp.where(order_row == source, 1.0, term)
        return factor

    def tables(step, carry):
        o1 = col_ref[step, 0:1, :]
        o2 = col_ref[step, 1:2, :]
        re = col_ref[step, 2:3, :]
        im = col_ref[step, 3:4, :]
        k1 = o1 + corner_first
        k2 = o2 + corner_second
        linear = m_scale * o1 + (o2 * (boxes_y / (2.0 * N)) + half_turn)
        root = jnp.sqrt(1.0 + sq_first * (k1 * k1) + sq_second * (k2 * k2))
        cosine, sine = cos_sin((linear - jnp.round(linear)) + root)
        hr_ref[step] = cosine * re - sine * im
        hi_ref[step] = cosine * im + sine * re
        cosine, sine = cos_sin(v_second * o2 - v_first * o1)
        zr_ref[step] = cosine
        zi_ref[step] = sine
        first = lagrange(o1 * (1.0 / wx))
        second = lagrange(o2 * (1.0 / wy))
        basis = jnp.concatenate([first[t : t + 1] * second for t in range(ORDER)], axis=0)
        half_turns = (4.0 * unit * (o2 - o1), -unit * (4.0 * o1 + 12.0 * o2))
        for side, cycles in enumerate(half_turns):
            cosine, sine = cos_sin(cycles)
            high, low = split(jnp.concatenate([basis * cosine, basis * sine], axis=0))
            basis_ref[side, step] = jnp.transpose(jnp.concatenate([high, low], axis=0))
        return carry

    lax.fori_loop(0, steps, tables, 0)

    def leaf(group):
        first_u = TGT1 // 2 + group * UC
        spans = (slice(0, WRAP), slice(WRAP, TGT2))

        def add(block, carry):
            parts = [0.0, 0.0]
            for inner in range(UNROLL):
                step = block * UNROLL + inner
                for side, span in enumerate(spans):
                    zr = zr_ref[step, span, :]
                    zi = zi_ref[step, span, :]
                    reals = []
                    imags = []
                    for u in range(first_u, first_u + UC):
                        start = HALF * (u % 2) + u // 2
                        hr = hr_ref[step, start + span.start : start + span.stop, :]
                        hi = hi_ref[step, start + span.start : start + span.stop, :]
                        reals.append(hr * zr - hi * zi)
                        imags.append(hr * zi + hi * zr)
                    high, low = split(jnp.concatenate(reals + imags, axis=0))
                    basis = basis_ref[side, step]
                    part = jnp.dot(high, basis, preferred_element_type=F32)
                    part = part + jnp.dot(low, basis, preferred_element_type=F32)
                    parts[side] = parts[side] + part
            acc_ref[: 2 * UC * WRAP] += parts[0]
            acc_ref[2 * UC * WRAP :] += parts[1]
            return carry

        acc_ref[...] = jnp.zeros_like(acc_ref)
        lax.fori_loop(0, steps // UNROLL, add, 0)
        summed = acc_ref[:, : 2 * NODES] + acc_ref[:, 2 * NODES :]
        rest = TGT2 - WRAP
        same = []
        turned = []
        for i in range(2 * UC):
            head = summed[i * WRAP : (i + 1) * WRAP]
            tail = summed[2 * UC * WRAP + i * rest : 2 * UC * WRAP + (i + 1) * rest]
            same += [head, tail]
            turned += [tail, head]
        same = jnp.transpose(jnp.concatenate(same, axis=0))
        turned = jnp.transpose(jnp.concatenate(turned, axis=0))
        upper = (
            same[:NODES, :CW] + same[NODES:, CW:],
            same[:NODES, CW:] - same[NODES:, :CW],
        )
        lower = (
            turned[:NODES, :CW] - turned[NODES:, CW:],
            turned[:NODES, CW:] + turned[NODES:, :CW],
        )
        return {group: lower, GROUPS + group: upper}

    lane = lax.broadcasted_iota(jnp.int32, (1, CW), 1)

    def centre(chunk, m1, m2):
        u = (lane // TGT2 + chunk * UC) * 2**m1 + code_of(ix, m1)
        v = lane % TGT2 * 2**m2 + code_of(iy, m2)
        first = (u.astype(F32) + 0.5) * (boxes_x / (N * 2.0**m1))
        second = (v.astype(F32) + 0.5) * (boxes_y / (N * 2.0**m2))
        return first, second

    def roots(place, n1, n2):
        wave = cos_sin(64.0 * (place[0] + place[1]))[1]
        first, second = speeds(wave)
        return jnp.sqrt(1.0 + (first * first) * (n1 * n1) + (second * second) * (n2 * n2))

    def box_nodes(px, py, m1, m2):
        a1 = (px // 2**m1 * (wx * 2**m1)).astype(F32)
        a2 = (py // 2**m2 * (wy * 2**m2)).astype(F32)
        n1 = a1 + float(wx * 2**m1) * first_nodes
        n2 = a2 + float(wy * 2**m2) * second_nodes
        return n1, n2

    def merge(chunk, stage, mine, other):
        level, along = stage // 2, stage % 2
        m1, m2 = level + along, level
        new1, new2 = (m1 + 1, m2) if along == 0 else (m1, m2 + 1)
        old_place = centre(chunk, m1, m2)
        new_place = centre(chunk, new1, new2)
        shift1 = (
            (code_of(ix, new1).astype(F32) + 0.5) * (boxes_x / (N * 2.0**new1))
            - (code_of(ix, m1).astype(F32) + 0.5) * (boxes_x / (N * 2.0**m1))
        )
        shift2 = (
            (code_of(iy, new2).astype(F32) + 0.5) * (boxes_y / (N * 2.0**new2))
            - (code_of(iy, m2).astype(F32) + 0.5) * (boxes_y / (N * 2.0**m2))
        )
        px = flipped(ix, level) if along == 0 else ix
        py = flipped(iy, level) if along == 1 else iy
        bit = ((ix if along == 0 else iy) // 2**level) % 2
        lifted = []
        for child, bx, by in ((mine, ix, iy), (other, px, py)):
            n1, n2 = box_nodes(bx, by, m1, m2)
            linear = shift1 * n1 + shift2 * n2
            cycles = (roots(new_place, n1, n2) - roots(old_place, n1, n2)) + linear
            cosine, sine = cos_sin(cycles)
            lifted.append(
                jnp.concatenate(
                    [cosine * child[0] - sine * child[1], cosine * child[1] + sine * child[0]],
                    axis=1,
                )
            )
        low, high = merge_ref[along, 0], merge_ref[along, 1]
        side = bit.astype(F32)
        table_mine = low * (1.0 - side) + high * side
        table_other = low * side + high * (1.0 - side)
        table = jnp.concatenate([table_mine, table_other], axis=1)
        table_high, table_low = split(table)
        high, low = split(jnp.concatenate(lifted, axis=0))
        total = jnp.dot(table_high, high, preferred_element_type=F32)
        total = total + jnp.dot(table_low, high, preferred_element_type=F32)
        total = total + jnp.dot(table_high, low, preferred_element_type=F32)
        return total[:, :CW], total[:, CW:]

    def finish(chunk, total):
        place = centre(chunk, 2, 2)
        n1, n2 = box_nodes(ix, iy, 2, 2)
        linear = place[0] * n1 + place[1] * n2
        cosine, sine = cos_sin((linear - jnp.round(linear)) + roots(place, n1, n2))
        lanes = slice(chunk * CW, (chunk + 1) * CW)
        out_ref[0, :, lanes] = cosine * total[0] + sine * total[1]
        out_ref[1, :, lanes] = cosine * total[1] - sine * total[0]

    def exchange(stage, chunk):
        return pltpu.make_async_remote_copy(
            src_ref=sent_ref.at[stage, chunk],
            dst_ref=got_ref.at[stage, chunk],
            send_sem=send_sem.at[stage, chunk],
            recv_sem=recv_sem.at[stage, chunk],
            device_id=partners[stage],
            device_id_type=MESH,
        )

    def send(stage, chunk, value):
        sent_ref[stage, chunk, 0] = value[0]
        sent_ref[stage, chunk, 1] = value[1]
        exchange(stage, chunk).start()

    greeted = False
    for slot in range(GROUPS + 4):
        if slot < GROUPS:
            values = leaf(slot)
            if not greeted:
                pl.semaphore_wait(barrier, 4)
                greeted = True
            for chunk, value in values.items():
                send(0, chunk, value)
        for stage in range(3, -1, -1):
            group = slot - 1 - stage
            if 0 <= group < GROUPS:
                for chunk in (group, GROUPS + group):
                    exchange(stage, chunk).wait()
                    value = merge(chunk, stage, sent_ref.at[stage, chunk], got_ref.at[stage, chunk])
                    if stage < 3:
                        send(stage + 1, chunk, value)
                    else:
                        finish(chunk, value)


def on_device(point_box, point_offset, point_value, coef):
    boxes_x = lax.axis_size("bx")
    boxes_y = lax.axis_size("by")
    assert boxes_y == 2 * boxes_x
    owners = boxes_x * boxes_y
    held = point_box.shape[0]
    cap = 2 * held // owners
    vmem = pl.BlockSpec(memory_space=pltpu.VMEM)
    block = (owners, 4 * cap // 128, 128)
    arrived = pl.pallas_call(
        functools.partial(pack_kernel, boxes_y, owners, cap),
        out_shape=jax.ShapeDtypeStruct(block, F32),
        in_specs=[pl.BlockSpec(memory_space=pl.ANY)] * 3,
        out_specs=vmem,
        scratch_shapes=[
            pltpu.VMEM((1, held), jnp.int32),
            pltpu.VMEM((2, held), jnp.int32),
            pltpu.VMEM((2, held), F32),
            pltpu.VMEM(block, F32),
            pltpu.VMEM(block, F32),
            pltpu.SemaphoreType.DMA((3,)),
            pltpu.SemaphoreType.DMA((owners,)),
            pltpu.SemaphoreType.DMA((owners,)),
        ],
        compiler_params=pltpu.CompilerParams(
            collective_id=1, has_side_effects=True, vmem_limit_bytes=16 << 20
        ),
        name="pack",
    )(point_box.reshape(1, held), point_offset, point_value)
    slots = owners * cap
    steps = slots // STEP
    columns = arrived.reshape(owners, 4, cap).transpose(1, 0, 2).reshape(4, steps, STEP)
    columns = columns.transpose(1, 0, 2)
    return pl.pallas_call(
        functools.partial(main_kernel, boxes_x, boxes_y),
        out_shape=jax.ShapeDtypeStruct((2, NODES, TGT1 * TGT2), F32),
        in_specs=[pl.BlockSpec(memory_space=pltpu.SMEM)] + [vmem] * 2,
        out_specs=vmem,
        scratch_shapes=[
            pltpu.VMEM((steps, 2 * HALF, STEP), F32),
            pltpu.VMEM((steps, 2 * HALF, STEP), F32),
            pltpu.VMEM((steps, TGT2, STEP), F32),
            pltpu.VMEM((steps, TGT2, STEP), F32),
            pltpu.VMEM((2, steps, STEP, 4 * NODES), BF16),
            pltpu.VMEM((2 * CW, 4 * NODES), F32),
            pltpu.VMEM((4, CHUNKS, 2, NODES, CW), F32),
            pltpu.VMEM((4, CHUNKS, 2, NODES, CW), F32),
            pltpu.SemaphoreType.DMA((4, CHUNKS)),
            pltpu.SemaphoreType.DMA((4, CHUNKS)),
        ],
        compiler_params=pltpu.CompilerParams(
            collective_id=0, has_side_effects=True, vmem_limit_bytes=40 << 20
        ),
        name="butterfly",
    )(coef, columns, jnp.asarray(merge_tables()))


def solution(mesh):
    in_specs = (P(("bx", "by"), None), P(None, ("bx", "by")), P(None, ("bx", "by")), P())
    out_specs = P(None, None, ("bx", "by"))
    return jax.shard_map(
        on_device, mesh=mesh, in_specs=in_specs, out_specs=out_specs, check_vma=False
    )
```

```python
import functools

import jax
import jax.numpy as jnp
import numpy as np
from jax import lax
from jax.experimental import pallas as pl
from jax.experimental.pallas import tpu as pltpu
from jax.sharding import PartitionSpec as P

N = 16384
ORDER = 8
NODES = ORDER * ORDER
TGT1 = 32
TGT2 = 32
STEP = 256
UC = 4
CW = UC * TGT2
CHUNKS = TGT1 // UC
GROUP = 2
GROUPS = CHUNKS // GROUP
WRAP = 24
UNROLL = 2
HALF = 48
MESH = pl.DeviceIdType.MESH
F32 = jnp.float32
BF16 = jnp.bfloat16
NT = (((1,), (1,)), ((), ()))


def node_table():
    counting = np.arange(ORDER) * 1.0
    return 0.5 - 0.5 * np.cos(np.pi * (2.0 * counting + 1.0) / (2.0 * ORDER))


def child_matrix(side):
    nodes = node_table()
    points = 0.5 * (side + nodes)
    rows_all = []
    for target in range(ORDER):
        factor = np.ones(ORDER)
        for source in range(ORDER):
            if source != target:
                factor = factor * (points - nodes[source]) / (nodes[target] - nodes[source])
        rows_all.append(factor)
    return np.stack(rows_all).astype(np.float32)


def merge_tables():
    eye = np.eye(ORDER, dtype=np.float32)
    first = [np.kron(child_matrix(side), eye) for side in (0, 1)]
    second = [np.kron(eye, child_matrix(side)) for side in (0, 1)]
    return np.stack([np.stack(first), np.stack(second)])


def lagrange_scales():
    nodes = node_table()
    scales = np.ones((ORDER, ORDER))
    for target in range(ORDER):
        for source in range(ORDER):
            if source != target:
                scales[target, source] = 1.0 / (nodes[target] - nodes[source])
    return scales.astype(np.float32)


def sine_coefficients():
    y = 0.25 * np.cos(np.pi * (np.arange(400) + 0.5) / 800)
    target = np.sin(2 * np.pi * y) / y
    fit = np.polynomial.chebyshev.Chebyshev.fit(y * y, target, 5, domain=[0.0, 1.0 / 16.0])
    return [float(c) for c in fit.convert(kind=np.polynomial.Polynomial).coef]


SINE = sine_coefficients()


def quarter_sine(y):
    square = y * y
    value = jnp.full_like(y, SINE[5])
    for c in SINE[4::-1]:
        value = value * square + c
    return value * y


def cos_sin(cycles):
    q = cycles - jnp.round(cycles)
    cosine = quarter_sine(0.25 - jnp.abs(q))
    sine = quarter_sine(jnp.maximum(jnp.minimum(q, 0.5 - q), -0.5 - q))
    return cosine, sine


def split(value):
    high = value.astype(BF16)
    return high, (value - high.astype(F32)).astype(BF16)


def pack_kernel(
    boxes_y, owners, cap, ids_hbm, offset_hbm, value_hbm, out_ref,
    ids_ref, offset_ref, value_ref, sent_ref, got_ref, load_sem, send_sem, recv_sem,
):
    me = lax.axis_index("bx") * boxes_y + lax.axis_index("by")
    barrier = pltpu.get_barrier_semaphore()
    loads = [
        pltpu.make_async_copy(ids_hbm, ids_ref, load_sem.at[0]),
        pltpu.make_async_copy(offset_hbm, offset_ref, load_sem.at[1]),
        pltpu.make_async_copy(value_hbm, value_ref, load_sem.at[2]),
    ]
    for load in loads:
        load.start()

    def place_of(distance):
        target = (me + distance) % owners
        return target, {"bx": target // boxes_y, "by": target % boxes_y}

    def greet(distance, carry):
        where = place_of(distance)[1]
        pl.semaphore_signal(barrier, inc=1, device_id=where, device_id_type=MESH)
        return carry

    lax.fori_loop(1, owners, greet, 0)
    total = ids_ref.shape[1]
    width = 256
    earlier = lax.broadcasted_iota(jnp.int32, (width, width), 0)
    later = lax.broadcasted_iota(jnp.int32, (width, width), 1)
    tri = (earlier < later).astype(F32).astype(BF16)
    carry = jnp.zeros((owners, 1), F32)
    for load in loads:
        load.wait()
    packed = jnp.zeros((10 * owners, cap), F32)
    for block in range(total // width):
        lanes = slice(block * width, (block + 1) * width)
        ids = ids_ref[:, lanes]
        hit = ids == lax.broadcasted_iota(jnp.int32, (owners, width), 0)
        onehot = hit.astype(F32)
        before = jnp.dot(onehot.astype(BF16), tri, preferred_element_type=F32) + carry
        ranks = jnp.sum(before * onehot, axis=0, keepdims=True)
        carry = carry + jnp.sum(onehot, axis=1, keepdims=True)
        slot = lax.broadcasted_iota(jnp.int32, (cap, width), 0)
        place = (slot == ranks.astype(jnp.int32)).astype(F32).astype(BF16)
        parts = []
        for row in range(2):
            offset = offset_ref[row : row + 1, lanes]
            low = offset & 127
            parts += [(offset - low).astype(F32), low.astype(F32)]
        for row in range(2):
            value = value_ref[row : row + 1, lanes]
            high = value.astype(BF16).astype(F32)
            rest = value - high
            middle = rest.astype(BF16).astype(F32)
            parts += [high, middle, rest - middle]
        lhs = jnp.concatenate([onehot * part for part in parts], axis=0).astype(BF16)
        packed = packed + lax.dot_general(lhs, place, NT, preferred_element_type=F32)
    rows = [packed[i * owners : (i + 1) * owners] for i in range(10)]
    fields = [rows[0] + rows[1], rows[2] + rows[3]]
    fields += [(rows[4] + rows[5]) + rows[6], (rows[7] + rows[8]) + rows[9]]
    joined = jnp.concatenate(fields, axis=1)
    for i in range(4 * cap // 128):
        sent_ref[:, i, :] = joined[:, i * 128 : (i + 1) * 128]

    def copy(distance):
        target, where = place_of(distance)
        return pltpu.make_async_remote_copy(
            src_ref=sent_ref.at[target],
            dst_ref=got_ref.at[me],
            send_sem=send_sem.at[distance],
            recv_sem=recv_sem.at[distance],
            device_id=where,
            device_id_type=MESH,
        )

    def begin(distance, carry):
        copy(distance).start()
        return carry

    def end(distance, carry):
        copy(distance).wait()
        return carry

    pl.semaphore_wait(barrier, owners - 1)
    lax.fori_loop(1, owners, begin, 0)
    got_ref[me] = sent_ref[me]
    lax.fori_loop(1, owners, end, 0)
    out_ref[...] = got_ref[...]


def code_of(index, merged):
    code = index * 0
    for bit in range(merged):
        code = code + (index // 2**bit) % 2 * 2 ** (merged - 1 - bit)
    return code


def flipped(index, level):
    return index + 2**level - 2 * 2**level * ((index // 2**level) % 2)


def main_kernel(
    boxes_x, boxes_y, coef_ref, col_ref, merge_ref, out_ref,
    hr_ref, hi_ref, zr_ref, zi_ref, basis_ref, acc_ref, ratio_ref, sent_ref, got_ref, send_sem, recv_sem,
):
    ix = lax.axis_index("bx")
    iy = lax.axis_index("by")
    partners = []
    for level in range(2):
        partners.append({"bx": flipped(ix, level), "by": iy})
        partners.append({"bx": ix, "by": flipped(iy, level)})
    barrier = pltpu.get_barrier_semaphore()
    for partner in partners:
        pl.semaphore_signal(barrier, inc=1, device_id=partner, device_id_type=MESH)

    wx = N // boxes_x
    wy = N // boxes_y
    steps = col_ref.shape[0]
    scaled = [coef_ref[i].astype(F32) for i in range(4)]

    def speeds(wave):
        first = (32.0 + scaled[0] + scaled[1] * wave) * (1.0 / 4096.0)
        second = (32.0 + scaled[2] + scaled[3] * wave) * (1.0 / 4096.0)
        return first, second

    row = lax.broadcasted_iota(jnp.int32, (2 * HALF, 1), 0)
    odd = (row >= HALF).astype(jnp.int32)
    m = (2 * (row - HALF * odd) + odd).astype(F32)
    wave = cos_sin(64.0 / N * ((m + 0.5) * boxes_x + 0.5 * boxes_y))[1]
    speed_first, speed_second = speeds(wave)
    sq_first = speed_first * speed_first
    sq_second = speed_second * speed_second
    m_scale = (2.0 * m + 1.0) * (boxes_x / (2.0 * N))
    v_row = lax.broadcasted_iota(jnp.int32, (TGT2, 1), 0)
    unit = boxes_y / N
    v_first = (v_row + 4).astype(F32) * unit
    v_second = jnp.where(v_row < WRAP, v_row + 4, v_row - 12).astype(F32) * unit
    half_turn = ((ix + iy) % 2).astype(F32) * 0.5
    corner_first = (ix * wx).astype(F32)
    corner_second = (iy * wy).astype(F32)
    node_values = node_table()
    order_row = lax.broadcasted_iota(jnp.int32, (ORDER, 1), 0)

    scales = lagrange_scales()

    def column(values):
        chosen = jnp.full((ORDER, 1), float(values[0]), F32)
        for i in range(1, ORDER):
            chosen = jnp.where(order_row == i, float(values[i]), chosen)
        return chosen

    scale_columns = [column(scales[:, source]) for source in range(ORDER)]
    tile_nodes = column(node_values)
    second_nodes = jnp.concatenate([tile_nodes] * ORDER, axis=0)
    first_nodes = jnp.concatenate(
        [jnp.full((ORDER, 1), float(node_values[t]), F32) for t in range(ORDER)], axis=0
    )

    def lagrange(coords):
        factor = jnp.ones((ORDER, STEP), F32)
        for source in range(ORDER):
            term = (coords - float(node_values[source])) * scale_columns[source]
            factor = factor * jnp.where(order_row == source, 1.0, term)
        return factor

    def tables(step, carry):
        o1 = col_ref[step, 0:1, :]
        o2 = col_ref[step, 1:2, :]
        re = col_ref[step, 2:3, :]
        im = col_ref[step, 3:4, :]
        k1 = o1 + corner_first
        k2 = o2 + corner_second
        linear = m_scale * o1 + (o2 * (boxes_y / (2.0 * N)) + half_turn)
        root = jnp.sqrt(1.0 + sq_first * (k1 * k1) + sq_second * (k2 * k2))
        cosine, sine = cos_sin((linear - jnp.round(linear)) + root)
        hr_ref[step] = cosine * re - sine * im
        hi_ref[step] = cosine * im + sine * re
        cosine, sine = cos_sin(v_second * o2 - v_first * o1)
        zr_ref[step] = cosine
        zi_ref[step] = sine
        first = lagrange(o1 * (1.0 / wx))
        second = lagrange(o2 * (1.0 / wy))
        basis = jnp.concatenate([first[t : t + 1] * second for t in range(ORDER)], axis=0)
        half_turns = (4.0 * unit * (o2 - o1), -unit * (4.0 * o1 + 12.0 * o2))
        for side, cycles in enumerate(half_turns):
            cosine, sine = cos_sin(cycles)
            high, low = split(jnp.concatenate([basis * cosine, basis * sine], axis=0))
            basis_ref[side, step] = jnp.transpose(jnp.concatenate([high, low], axis=0))
        return carry

    lax.fori_loop(0, steps, tables, 0)

    def leaf(group):
        first_u = TGT1 // 2 + group * UC
        spans = (slice(0, WRAP), slice(WRAP, TGT2))

        def add(block, carry):
            parts = [0.0, 0.0]
            for inner in range(UNROLL):
                step = block * UNROLL + inner
                for side, span in enumerate(spans):
                    zr = zr_ref[step, span, :]
                    zi = zi_ref[step, span, :]
                    reals = []
                    imags = []
                    for u in range(first_u, first_u + UC):
                        start = HALF * (u % 2) + u // 2
                        hr = hr_ref[step, start + span.start : start + span.stop, :]
                        hi = hi_ref[step, start + span.start : start + span.stop, :]
                        reals.append(hr * zr - hi * zi)
                        imags.append(hr * zi + hi * zr)
                    high, low = split(jnp.concatenate(reals + imags, axis=0))
                    basis = basis_ref[side, step]
                    part = jnp.dot(high, basis, preferred_element_type=F32)
                    part = part + jnp.dot(low, basis, preferred_element_type=F32)
                    parts[side] = parts[side] + part
            acc_ref[: 2 * UC * WRAP] += parts[0]
            acc_ref[2 * UC * WRAP :] += parts[1]
            return carry

        acc_ref[...] = jnp.zeros_like(acc_ref)
        lax.fori_loop(0, steps // UNROLL, add, 0)
        summed = acc_ref[:, : 2 * NODES] + acc_ref[:, 2 * NODES :]
        rest = TGT2 - WRAP
        same = []
        turned = []
        for i in range(2 * UC):
            head = summed[i * WRAP : (i + 1) * WRAP]
            tail = summed[2 * UC * WRAP + i * rest : 2 * UC * WRAP + (i + 1) * rest]
            same += [head, tail]
            turned += [tail, head]
        same = jnp.transpose(jnp.concatenate(same, axis=0))
        turned = jnp.transpose(jnp.concatenate(turned, axis=0))
        upper = (
            same[:NODES, :CW] + same[NODES:, CW:],
            same[:NODES, CW:] - same[NODES:, :CW],
        )
        lower = (
            turned[:NODES, :CW] - turned[NODES:, CW:],
            turned[:NODES, CW:] + turned[NODES:, :CW],
        )
        return {group: lower, GROUPS + group: upper}

    lane = lax.broadcasted_iota(jnp.int32, (1, CW), 1)

    def centre(chunk, m1, m2):
        u = (lane // TGT2 + chunk * UC) * 2**m1 + code_of(ix, m1)
        v = lane % TGT2 * 2**m2 + code_of(iy, m2)
        first = (u.astype(F32) + 0.5) * (boxes_x / (N * 2.0**m1))
        second = (v.astype(F32) + 0.5) * (boxes_y / (N * 2.0**m2))
        return first, second

    def roots(place, n1, n2):
        wave = cos_sin(64.0 * (place[0] + place[1]))[1]
        first, second = speeds(wave)
        return jnp.sqrt(1.0 + (first * first) * (n1 * n1) + (second * second) * (n2 * n2))

    def box_nodes(px, py, m1, m2):
        a1 = (px // 2**m1 * (wx * 2**m1)).astype(F32)
        a2 = (py // 2**m2 * (wy * 2**m2)).astype(F32)
        n1 = a1 + float(wx * 2**m1) * first_nodes
        n2 = a2 + float(wy * 2**m2) * second_nodes
        return n1, n2

    def ratios(stage):
        level, along = stage // 2, stage % 2
        m1, m2 = level + along, level
        new1, new2 = (m1 + 1, m2) if along == 0 else (m1, m2 + 1)
        old_place = centre(0, m1, m2)
        new_place = centre(0, new1, new2)
        shift1 = (
            (code_of(ix, new1).astype(F32) + 0.5) * (boxes_x / (N * 2.0**new1))
            - (code_of(ix, m1).astype(F32) + 0.5) * (boxes_x / (N * 2.0**m1))
        )
        shift2 = (
            (code_of(iy, new2).astype(F32) + 0.5) * (boxes_y / (N * 2.0**new2))
            - (code_of(iy, m2).astype(F32) + 0.5) * (boxes_y / (N * 2.0**m2))
        )
        px = flipped(ix, level) if along == 0 else ix
        py = flipped(iy, level) if along == 1 else iy
        for child, (bx, by) in enumerate(((ix, iy), (px, py))):
            n1, n2 = box_nodes(bx, by, m1, m2)
            linear = shift1 * n1 + shift2 * n2
            cycles = (roots(new_place, n1, n2) - roots(old_place, n1, n2)) + linear
            cosine, sine = cos_sin(cycles)
            ratio_ref[stage, child, 0] = cosine
            ratio_ref[stage, child, 1] = sine

    def turned_ratio(stage, child, chunk):
        turn = 2 * chunk
        for part in range(2):
            value = ratio_ref[stage, child, part]
            if turn:
                near = pltpu.roll(value, CW - turn, 1)
                far = pltpu.roll(value, TGT2 - turn, 1)
                value = jnp.where(lane % TGT2 + turn < TGT2, near, far)
            yield value

    def merge(chunk, stage, mine, other):
        level, along = stage // 2, stage % 2
        bit = ((ix if along == 0 else iy) // 2**level) % 2
        lifted = []
        for index, child in enumerate((mine, other)):
            cosine, sine = turned_ratio(stage, index, chunk)
            lifted.append(
                jnp.concatenate(
                    [cosine * child[0] - sine * child[1], cosine * child[1] + sine * child[0]],
                    axis=1,
                )
            )
        low, high = merge_ref[along, 0], merge_ref[along, 1]
        side = bit.astype(F32)
        table_mine = low * (1.0 - side) + high * side
        table_other = low * side + high * (1.0 - side)
        table = jnp.concatenate([table_mine, table_other], axis=1)
        table_high, table_low = split(table)
        high, low = split(jnp.concatenate(lifted, axis=0))
        total = jnp.dot(table_high, high, preferred_element_type=F32)
        total = total + jnp.dot(table_low, high, preferred_element_type=F32)
        total = total + jnp.dot(table_high, low, preferred_element_type=F32)
        return total[:, :CW], total[:, CW:]

    def finish(chunk, total):
        place = centre(chunk, 2, 2)
        n1, n2 = box_nodes(ix, iy, 2, 2)
        linear = place[0] * n1 + place[1] * n2
        cosine, sine = cos_sin((linear - jnp.round(linear)) + roots(place, n1, n2))
        lanes = slice(chunk * CW, (chunk + 1) * CW)
        out_ref[0, :, lanes] = cosine * total[0] + sine * total[1]
        out_ref[1, :, lanes] = cosine * total[1] - sine * total[0]

    def exchange(stage, chunk):
        return pltpu.make_async_remote_copy(
            src_ref=sent_ref.at[stage, chunk],
            dst_ref=got_ref.at[stage, chunk],
            send_sem=send_sem.at[stage, chunk],
            recv_sem=recv_sem.at[stage, chunk],
            device_id=partners[stage],
            device_id_type=MESH,
        )

    def send(stage, chunk, value):
        sent_ref[stage, chunk, 0] = value[0]
        sent_ref[stage, chunk, 1] = value[1]
        exchange(stage, chunk).start()

    for stage in range(4):
        ratios(stage)
    greeted = False
    for slot in range(GROUPS + 4):
        if slot < GROUPS:
            values = leaf(slot)
            if not greeted:
                pl.semaphore_wait(barrier, 4)
                greeted = True
            for chunk, value in values.items():
                send(0, chunk, value)
        for stage in range(3, -1, -1):
            group = slot - 1 - stage
            if 0 <= group < GROUPS:
                for chunk in (group, GROUPS + group):
                    exchange(stage, chunk).wait()
                    value = merge(chunk, stage, sent_ref.at[stage, chunk], got_ref.at[stage, chunk])
                    if stage < 3:
                        send(stage + 1, chunk, value)
                    else:
                        finish(chunk, value)


def on_device(point_box, point_offset, point_value, coef):
    boxes_x = lax.axis_size("bx")
    boxes_y = lax.axis_size("by")
    assert boxes_y == 2 * boxes_x
    owners = boxes_x * boxes_y
    held = point_box.shape[0]
    cap = 2 * held // owners
    vmem = pl.BlockSpec(memory_space=pltpu.VMEM)
    block = (owners, 4 * cap // 128, 128)
    arrived = pl.pallas_call(
        functools.partial(pack_kernel, boxes_y, owners, cap),
        out_shape=jax.ShapeDtypeStruct(block, F32),
        in_specs=[pl.BlockSpec(memory_space=pl.ANY)] * 3,
        out_specs=vmem,
        scratch_shapes=[
            pltpu.VMEM((1, held), jnp.int32),
            pltpu.VMEM((2, held), jnp.int32),
            pltpu.VMEM((2, held), F32),
            pltpu.VMEM(block, F32),
            pltpu.VMEM(block, F32),
            pltpu.SemaphoreType.DMA((3,)),
            pltpu.SemaphoreType.DMA((owners,)),
            pltpu.SemaphoreType.DMA((owners,)),
        ],
        compiler_params=pltpu.CompilerParams(
            collective_id=1, has_side_effects=True, vmem_limit_bytes=16 << 20
        ),
        name="pack",
    )(point_box.reshape(1, held), point_offset, point_value)
    slots = owners * cap
    steps = slots // STEP
    columns = arrived.reshape(owners, 4, cap).transpose(1, 0, 2).reshape(4, steps, STEP)
    columns = columns.transpose(1, 0, 2)
    return pl.pallas_call(
        functools.partial(main_kernel, boxes_x, boxes_y),
        out_shape=jax.ShapeDtypeStruct((2, NODES, TGT1 * TGT2), F32),
        in_specs=[pl.BlockSpec(memory_space=pltpu.SMEM)] + [vmem] * 2,
        out_specs=vmem,
        scratch_shapes=[
            pltpu.VMEM((steps, 2 * HALF, STEP), F32),
            pltpu.VMEM((steps, 2 * HALF, STEP), F32),
            pltpu.VMEM((steps, TGT2, STEP), F32),
            pltpu.VMEM((steps, TGT2, STEP), F32),
            pltpu.VMEM((2, steps, STEP, 4 * NODES), BF16),
            pltpu.VMEM((2 * CW, 4 * NODES), F32),
            pltpu.VMEM((4, 2, 2, NODES, CW), F32),
            pltpu.VMEM((4, CHUNKS, 2, NODES, CW), F32),
            pltpu.VMEM((4, CHUNKS, 2, NODES, CW), F32),
            pltpu.SemaphoreType.DMA((4, CHUNKS)),
            pltpu.SemaphoreType.DMA((4, CHUNKS)),
        ],
        compiler_params=pltpu.CompilerParams(
            collective_id=0, has_side_effects=True, vmem_limit_bytes=40 << 20
        ),
        name="butterfly",
    )(coef, columns, jnp.asarray(merge_tables()))


def solution(mesh):
    in_specs = (P(("bx", "by"), None), P(None, ("bx", "by")), P(None, ("bx", "by")), P())
    out_specs = P(None, None, ("bx", "by"))
    return jax.shard_map(
        on_device, mesh=mesh, in_specs=in_specs, out_specs=out_specs, check_vma=False
    )
```

```python
import functools

import jax
import jax.numpy as jnp
import numpy as np
from jax import lax
from jax.experimental import pallas as pl
from jax.experimental.pallas import tpu as pltpu
from jax.sharding import PartitionSpec as P

N = 16384
ORDER = 8
NODES = ORDER * ORDER
TGT1 = 32
TGT2 = 32
STEP = 256
UC = 4
CW = UC * TGT2
CHUNKS = TGT1 // UC
GROUP = 2
GROUPS = CHUNKS // GROUP
WRAP = 24
UNROLL = 4
HALF = 48
MESH = pl.DeviceIdType.MESH
F32 = jnp.float32
BF16 = jnp.bfloat16
NT = (((1,), (1,)), ((), ()))


def node_table():
    counting = np.arange(ORDER) * 1.0
    return 0.5 - 0.5 * np.cos(np.pi * (2.0 * counting + 1.0) / (2.0 * ORDER))


def child_matrix(side):
    nodes = node_table()
    points = 0.5 * (side + nodes)
    rows_all = []
    for target in range(ORDER):
        factor = np.ones(ORDER)
        for source in range(ORDER):
            if source != target:
                factor = factor * (points - nodes[source]) / (nodes[target] - nodes[source])
        rows_all.append(factor)
    return np.stack(rows_all).astype(np.float32)


def merge_tables():
    eye = np.eye(ORDER, dtype=np.float32)
    first = [np.kron(child_matrix(side), eye) for side in (0, 1)]
    second = [np.kron(eye, child_matrix(side)) for side in (0, 1)]
    return np.stack([np.stack(first), np.stack(second)])


def lagrange_scales():
    nodes = node_table()
    scales = np.ones((ORDER, ORDER))
    for target in range(ORDER):
        for source in range(ORDER):
            if source != target:
                scales[target, source] = 1.0 / (nodes[target] - nodes[source])
    return scales.astype(np.float32)


def sine_coefficients():
    y = 0.25 * np.cos(np.pi * (np.arange(400) + 0.5) / 800)
    target = np.sin(2 * np.pi * y) / y
    fit = np.polynomial.chebyshev.Chebyshev.fit(y * y, target, 5, domain=[0.0, 1.0 / 16.0])
    return [float(c) for c in fit.convert(kind=np.polynomial.Polynomial).coef]


SINE = sine_coefficients()


def quarter_sine(y):
    square = y * y
    value = jnp.full_like(y, SINE[5])
    for c in SINE[4::-1]:
        value = value * square + c
    return value * y


def cos_sin(cycles):
    q = cycles - jnp.round(cycles)
    cosine = quarter_sine(0.25 - jnp.abs(q))
    sine = quarter_sine(jnp.maximum(jnp.minimum(q, 0.5 - q), -0.5 - q))
    return cosine, sine


def split(value):
    high = value.astype(BF16)
    return high, (value - high.astype(F32)).astype(BF16)


def pack_kernel(
    boxes_y, owners, cap, ids_hbm, offset_hbm, value_hbm, out_ref,
    ids_ref, offset_ref, value_ref, sent_ref, got_ref, load_sem, send_sem, recv_sem,
):
    me = lax.axis_index("bx") * boxes_y + lax.axis_index("by")
    barrier = pltpu.get_barrier_semaphore()
    loads = [
        pltpu.make_async_copy(ids_hbm, ids_ref, load_sem.at[0]),
        pltpu.make_async_copy(offset_hbm, offset_ref, load_sem.at[1]),
        pltpu.make_async_copy(value_hbm, value_ref, load_sem.at[2]),
    ]
    for load in loads:
        load.start()

    def place_of(distance):
        target = (me + distance) % owners
        return target, {"bx": target // boxes_y, "by": target % boxes_y}

    def greet(distance, carry):
        where = place_of(distance)[1]
        pl.semaphore_signal(barrier, inc=1, device_id=where, device_id_type=MESH)
        return carry

    lax.fori_loop(1, owners, greet, 0)
    total = ids_ref.shape[1]
    width = 256
    earlier = lax.broadcasted_iota(jnp.int32, (width, width), 0)
    later = lax.broadcasted_iota(jnp.int32, (width, width), 1)
    tri = (earlier < later).astype(F32).astype(BF16)
    carry = jnp.zeros((owners, 1), F32)
    for load in loads:
        load.wait()
    packed = jnp.zeros((10 * owners, cap), F32)
    for block in range(total // width):
        lanes = slice(block * width, (block + 1) * width)
        ids = ids_ref[:, lanes]
        hit = ids == lax.broadcasted_iota(jnp.int32, (owners, width), 0)
        onehot = hit.astype(F32)
        before = jnp.dot(onehot.astype(BF16), tri, preferred_element_type=F32) + carry
        ranks = jnp.sum(before * onehot, axis=0, keepdims=True)
        carry = carry + jnp.sum(onehot, axis=1, keepdims=True)
        slot = lax.broadcasted_iota(jnp.int32, (cap, width), 0)
        place = (slot == ranks.astype(jnp.int32)).astype(F32).astype(BF16)
        parts = []
        for row in range(2):
            offset = offset_ref[row : row + 1, lanes]
            low = offset & 127
            parts += [(offset - low).astype(F32), low.astype(F32)]
        for row in range(2):
            value = value_ref[row : row + 1, lanes]
            high = value.astype(BF16).astype(F32)
            rest = value - high
            middle = rest.astype(BF16).astype(F32)
            parts += [high, middle, rest - middle]
        lhs = jnp.concatenate([onehot * part for part in parts], axis=0).astype(BF16)
        packed = packed + lax.dot_general(lhs, place, NT, preferred_element_type=F32)
    rows = [packed[i * owners : (i + 1) * owners] for i in range(10)]
    fields = [rows[0] + rows[1], rows[2] + rows[3]]
    fields += [(rows[4] + rows[5]) + rows[6], (rows[7] + rows[8]) + rows[9]]
    joined = jnp.concatenate(fields, axis=1)
    for i in range(4 * cap // 128):
        sent_ref[:, i, :] = joined[:, i * 128 : (i + 1) * 128]

    def copy(distance):
        target, where = place_of(distance)
        return pltpu.make_async_remote_copy(
            src_ref=sent_ref.at[target],
            dst_ref=got_ref.at[me],
            send_sem=send_sem.at[distance],
            recv_sem=recv_sem.at[distance],
            device_id=where,
            device_id_type=MESH,
        )

    def begin(distance, carry):
        copy(distance).start()
        return carry

    def end(distance, carry):
        copy(distance).wait()
        return carry

    pl.semaphore_wait(barrier, owners - 1)
    lax.fori_loop(1, owners, begin, 0)
    got_ref[me] = sent_ref[me]
    lax.fori_loop(1, owners, end, 0)
    out_ref[...] = got_ref[...]


def code_of(index, merged):
    code = index * 0
    for bit in range(merged):
        code = code + (index // 2**bit) % 2 * 2 ** (merged - 1 - bit)
    return code


def flipped(index, level):
    return index + 2**level - 2 * 2**level * ((index // 2**level) % 2)


def main_kernel(
    boxes_x, boxes_y, coef_ref, col_ref, merge_ref, out_ref,
    hr_ref, hi_ref, zr_ref, zi_ref, basis_ref, acc_ref, ratio_ref, sent_ref, got_ref, send_sem, recv_sem,
):
    ix = lax.axis_index("bx")
    iy = lax.axis_index("by")
    partners = []
    for level in range(2):
        partners.append({"bx": flipped(ix, level), "by": iy})
        partners.append({"bx": ix, "by": flipped(iy, level)})
    barrier = pltpu.get_barrier_semaphore()
    for partner in partners:
        pl.semaphore_signal(barrier, inc=1, device_id=partner, device_id_type=MESH)

    wx = N // boxes_x
    wy = N // boxes_y
    steps = col_ref.shape[0]
    scaled = [coef_ref[i].astype(F32) for i in range(4)]

    def speeds(wave):
        first = (32.0 + scaled[0] + scaled[1] * wave) * (1.0 / 4096.0)
        second = (32.0 + scaled[2] + scaled[3] * wave) * (1.0 / 4096.0)
        return first, second

    row = lax.broadcasted_iota(jnp.int32, (2 * HALF, 1), 0)
    odd = (row >= HALF).astype(jnp.int32)
    m = (2 * (row - HALF * odd) + odd).astype(F32)
    wave = cos_sin(64.0 / N * ((m + 0.5) * boxes_x + 0.5 * boxes_y))[1]
    speed_first, speed_second = speeds(wave)
    sq_first = speed_first * speed_first
    sq_second = speed_second * speed_second
    m_scale = (2.0 * m + 1.0) * (boxes_x / (2.0 * N))
    v_row = lax.broadcasted_iota(jnp.int32, (TGT2, 1), 0)
    unit = boxes_y / N
    v_first = (v_row + 4).astype(F32) * unit
    v_second = jnp.where(v_row < WRAP, v_row + 4, v_row - 12).astype(F32) * unit
    half_turn = ((ix + iy) % 2).astype(F32) * 0.5
    corner_first = (ix * wx).astype(F32)
    corner_second = (iy * wy).astype(F32)
    node_values = node_table()
    order_row = lax.broadcasted_iota(jnp.int32, (ORDER, 1), 0)

    scales = lagrange_scales()

    def column(values):
        chosen = jnp.full((ORDER, 1), float(values[0]), F32)
        for i in range(1, ORDER):
            chosen = jnp.where(order_row == i, float(values[i]), chosen)
        return chosen

    scale_columns = [column(scales[:, source]) for source in range(ORDER)]
    tile_nodes = column(node_values)
    second_nodes = jnp.concatenate([tile_nodes] * ORDER, axis=0)
    first_nodes = jnp.concatenate(
        [jnp.full((ORDER, 1), float(node_values[t]), F32) for t in range(ORDER)], axis=0
    )

    def lagrange(coords):
        factor = jnp.ones((ORDER, STEP), F32)
        for source in range(ORDER):
            term = (coords - float(node_values[source])) * scale_columns[source]
            factor = factor * jnp.where(order_row == source, 1.0, term)
        return factor

    def tables(step, carry):
        o1 = col_ref[step, 0:1, :]
        o2 = col_ref[step, 1:2, :]
        re = col_ref[step, 2:3, :]
        im = col_ref[step, 3:4, :]
        k1 = o1 + corner_first
        k2 = o2 + corner_second
        linear = m_scale * o1 + (o2 * (boxes_y / (2.0 * N)) + half_turn)
        root = jnp.sqrt(1.0 + sq_first * (k1 * k1) + sq_second * (k2 * k2))
        cosine, sine = cos_sin((linear - jnp.round(linear)) + root)
        hr_ref[step] = cosine * re - sine * im
        hi_ref[step] = cosine * im + sine * re
        cosine, sine = cos_sin(v_second * o2 - v_first * o1)
        zr_ref[step] = cosine
        zi_ref[step] = sine
        first = lagrange(o1 * (1.0 / wx))
        second = lagrange(o2 * (1.0 / wy))
        basis = jnp.concatenate([first[t : t + 1] * second for t in range(ORDER)], axis=0)
        half_turns = (4.0 * unit * (o2 - o1), -unit * (4.0 * o1 + 12.0 * o2))
        for side, cycles in enumerate(half_turns):
            cosine, sine = cos_sin(cycles)
            high, low = split(jnp.concatenate([basis * cosine, basis * sine], axis=0))
            basis_ref[side, step] = jnp.transpose(jnp.concatenate([high, low], axis=0))
        return carry

    lax.fori_loop(0, steps, tables, 0)

    def leaf(group):
        first_u = TGT1 // 2 + group * UC
        spans = (slice(0, WRAP), slice(WRAP, TGT2))

        def add(block, carry):
            parts = [0.0, 0.0]
            for inner in range(UNROLL):
                step = block * UNROLL + inner
                for side, span in enumerate(spans):
                    zr = zr_ref[step, span, :]
                    zi = zi_ref[step, span, :]
                    reals = []
                    imags = []
                    for u in range(first_u, first_u + UC):
                        start = HALF * (u % 2) + u // 2
                        hr = hr_ref[step, start + span.start : start + span.stop, :]
                        hi = hi_ref[step, start + span.start : start + span.stop, :]
                        reals.append(hr * zr - hi * zi)
                        imags.append(hr * zi + hi * zr)
                    high, low = split(jnp.concatenate(reals + imags, axis=0))
                    basis = basis_ref[side, step]
                    part = jnp.dot(high, basis, preferred_element_type=F32)
                    part = part + jnp.dot(low, basis, preferred_element_type=F32)
                    parts[side] = parts[side] + part
            acc_ref[: 2 * UC * WRAP] += parts[0]
            acc_ref[2 * UC * WRAP :] += parts[1]
            return carry

        acc_ref[...] = jnp.zeros_like(acc_ref)
        lax.fori_loop(0, steps // UNROLL, add, 0)
        summed = acc_ref[:, : 2 * NODES] + acc_ref[:, 2 * NODES :]
        rest = TGT2 - WRAP
        same = []
        turned = []
        for i in range(2 * UC):
            head = summed[i * WRAP : (i + 1) * WRAP]
            tail = summed[2 * UC * WRAP + i * rest : 2 * UC * WRAP + (i + 1) * rest]
            same += [head, tail]
            turned += [tail, head]
        same = jnp.transpose(jnp.concatenate(same, axis=0))
        turned = jnp.transpose(jnp.concatenate(turned, axis=0))
        upper = (
            same[:NODES, :CW] + same[NODES:, CW:],
            same[:NODES, CW:] - same[NODES:, :CW],
        )
        lower = (
            turned[:NODES, :CW] - turned[NODES:, CW:],
            turned[:NODES, CW:] + turned[NODES:, :CW],
        )
        return {group: lower, GROUPS + group: upper}

    lane = lax.broadcasted_iota(jnp.int32, (1, CW), 1)

    def centre(chunk, m1, m2):
        u = (lane // TGT2 + chunk * UC) * 2**m1 + code_of(ix, m1)
        v = lane % TGT2 * 2**m2 + code_of(iy, m2)
        first = (u.astype(F32) + 0.5) * (boxes_x / (N * 2.0**m1))
        second = (v.astype(F32) + 0.5) * (boxes_y / (N * 2.0**m2))
        return first, second

    def roots(place, n1, n2):
        wave = cos_sin(64.0 * (place[0] + place[1]))[1]
        first, second = speeds(wave)
        return jnp.sqrt(1.0 + (first * first) * (n1 * n1) + (second * second) * (n2 * n2))

    def box_nodes(px, py, m1, m2):
        a1 = (px // 2**m1 * (wx * 2**m1)).astype(F32)
        a2 = (py // 2**m2 * (wy * 2**m2)).astype(F32)
        n1 = a1 + float(wx * 2**m1) * first_nodes
        n2 = a2 + float(wy * 2**m2) * second_nodes
        return n1, n2

    def ratios(stage):
        level, along = stage // 2, stage % 2
        m1, m2 = level + along, level
        new1, new2 = (m1 + 1, m2) if along == 0 else (m1, m2 + 1)
        old_place = centre(0, m1, m2)
        new_place = centre(0, new1, new2)
        shift1 = (
            (code_of(ix, new1).astype(F32) + 0.5) * (boxes_x / (N * 2.0**new1))
            - (code_of(ix, m1).astype(F32) + 0.5) * (boxes_x / (N * 2.0**m1))
        )
        shift2 = (
            (code_of(iy, new2).astype(F32) + 0.5) * (boxes_y / (N * 2.0**new2))
            - (code_of(iy, m2).astype(F32) + 0.5) * (boxes_y / (N * 2.0**m2))
        )
        px = flipped(ix, level) if along == 0 else ix
        py = flipped(iy, level) if along == 1 else iy
        for child, (bx, by) in enumerate(((ix, iy), (px, py))):
            n1, n2 = box_nodes(bx, by, m1, m2)
            linear = shift1 * n1 + shift2 * n2
            cycles = (roots(new_place, n1, n2) - roots(old_place, n1, n2)) + linear
            cosine, sine = cos_sin(cycles)
            ratio_ref[stage, child, 0] = cosine
            ratio_ref[stage, child, 1] = sine

    def turned_ratio(stage, child, chunk):
        turn = 2 * chunk
        for part in range(2):
            value = ratio_ref[stage, child, part]
            if turn:
                near = pltpu.roll(value, CW - turn, 1)
                far = pltpu.roll(value, TGT2 - turn, 1)
                value = jnp.where(lane % TGT2 + turn < TGT2, near, far)
            yield value

    def merge(chunk, stage, mine, other):
        level, along = stage // 2, stage % 2
        bit = ((ix if along == 0 else iy) // 2**level) % 2
        lifted = []
        for index, child in enumerate((mine, other)):
            cosine, sine = turned_ratio(stage, index, chunk)
            lifted.append(
                jnp.concatenate(
                    [cosine * child[0] - sine * child[1], cosine * child[1] + sine * child[0]],
                    axis=1,
                )
            )
        low, high = merge_ref[along, 0], merge_ref[along, 1]
        side = bit.astype(F32)
        table_mine = low * (1.0 - side) + high * side
        table_other = low * side + high * (1.0 - side)
        table = jnp.concatenate([table_mine, table_other], axis=1)
        table_high, table_low = split(table)
        high, low = split(jnp.concatenate(lifted, axis=0))
        total = jnp.dot(table_high, high, preferred_element_type=F32)
        total = total + jnp.dot(table_low, high, preferred_element_type=F32)
        total = total + jnp.dot(table_high, low, preferred_element_type=F32)
        return total[:, :CW], total[:, CW:]

    def finish(chunk, total):
        place = centre(chunk, 2, 2)
        n1, n2 = box_nodes(ix, iy, 2, 2)
        linear = place[0] * n1 + place[1] * n2
        cosine, sine = cos_sin((linear - jnp.round(linear)) + roots(place, n1, n2))
        lanes = slice(chunk * CW, (chunk + 1) * CW)
        out_ref[0, :, lanes] = cosine * total[0] + sine * total[1]
        out_ref[1, :, lanes] = cosine * total[1] - sine * total[0]

    def exchange(stage, chunk):
        return pltpu.make_async_remote_copy(
            src_ref=sent_ref.at[stage, chunk],
            dst_ref=got_ref.at[stage, chunk],
            send_sem=send_sem.at[stage, chunk],
            recv_sem=recv_sem.at[stage, chunk],
            device_id=partners[stage],
            device_id_type=MESH,
        )

    def send(stage, chunk, value):
        sent_ref[stage, chunk, 0] = value[0]
        sent_ref[stage, chunk, 1] = value[1]
        exchange(stage, chunk).start()

    for stage in range(4):
        ratios(stage)
    greeted = False
    for slot in range(GROUPS + 4):
        if slot < GROUPS:
            values = leaf(slot)
            if not greeted:
                pl.semaphore_wait(barrier, 4)
                greeted = True
            for chunk, value in values.items():
                send(0, chunk, value)
        for stage in range(3, -1, -1):
            group = slot - 1 - stage
            if 0 <= group < GROUPS:
                for chunk in (group, GROUPS + group):
                    exchange(stage, chunk).wait()
                    value = merge(chunk, stage, sent_ref.at[stage, chunk], got_ref.at[stage, chunk])
                    if stage < 3:
                        send(stage + 1, chunk, value)
                    else:
                        finish(chunk, value)


def on_device(point_box, point_offset, point_value, coef):
    boxes_x = lax.axis_size("bx")
    boxes_y = lax.axis_size("by")
    assert boxes_y == 2 * boxes_x
    owners = boxes_x * boxes_y
    held = point_box.shape[0]
    cap = 2 * held // owners
    vmem = pl.BlockSpec(memory_space=pltpu.VMEM)
    block = (owners, 4 * cap // 128, 128)
    arrived = pl.pallas_call(
        functools.partial(pack_kernel, boxes_y, owners, cap),
        out_shape=jax.ShapeDtypeStruct(block, F32),
        in_specs=[pl.BlockSpec(memory_space=pl.ANY)] * 3,
        out_specs=vmem,
        scratch_shapes=[
            pltpu.VMEM((1, held), jnp.int32),
            pltpu.VMEM((2, held), jnp.int32),
            pltpu.VMEM((2, held), F32),
            pltpu.VMEM(block, F32),
            pltpu.VMEM(block, F32),
            pltpu.SemaphoreType.DMA((3,)),
            pltpu.SemaphoreType.DMA((owners,)),
            pltpu.SemaphoreType.DMA((owners,)),
        ],
        compiler_params=pltpu.CompilerParams(
            collective_id=1, has_side_effects=True, vmem_limit_bytes=16 << 20
        ),
        name="pack",
    )(point_box.reshape(1, held), point_offset, point_value)
    slots = owners * cap
    steps = slots // STEP
    columns = arrived.reshape(owners, 4, cap).transpose(1, 0, 2).reshape(4, steps, STEP)
    columns = columns.transpose(1, 0, 2)
    return pl.pallas_call(
        functools.partial(main_kernel, boxes_x, boxes_y),
        out_shape=jax.ShapeDtypeStruct((2, NODES, TGT1 * TGT2), F32),
        in_specs=[pl.BlockSpec(memory_space=pltpu.SMEM)] + [vmem] * 2,
        out_specs=vmem,
        scratch_shapes=[
            pltpu.VMEM((steps, 2 * HALF, STEP), F32),
            pltpu.VMEM((steps, 2 * HALF, STEP), F32),
            pltpu.VMEM((steps, TGT2, STEP), F32),
            pltpu.VMEM((steps, TGT2, STEP), F32),
            pltpu.VMEM((2, steps, STEP, 4 * NODES), BF16),
            pltpu.VMEM((2 * CW, 4 * NODES), F32),
            pltpu.VMEM((4, 2, 2, NODES, CW), F32),
            pltpu.VMEM((4, CHUNKS, 2, NODES, CW), F32),
            pltpu.VMEM((4, CHUNKS, 2, NODES, CW), F32),
            pltpu.SemaphoreType.DMA((4, CHUNKS)),
            pltpu.SemaphoreType.DMA((4, CHUNKS)),
        ],
        compiler_params=pltpu.CompilerParams(
            collective_id=0, has_side_effects=True, vmem_limit_bytes=40 << 20
        ),
        name="butterfly",
    )(coef, columns, jnp.asarray(merge_tables()))


def solution(mesh):
    in_specs = (P(("bx", "by"), None), P(None, ("bx", "by")), P(None, ("bx", "by")), P())
    out_specs = P(None, None, ("bx", "by"))
    return jax.shard_map(
        on_device, mesh=mesh, in_specs=in_specs, out_specs=out_specs, check_vma=False
    )
```
